256 devices in a mesh: lat: 8 (over y, x_lo), lon: 32 (over x_hi, z, core).
Axes of the slice: x: 4 (x_hi: 2, x_lo: 2; x = x_hi * 2 + x_lo), y: 4, z: 8, core: 2. Of those that a mesh axis runs over, the one named last changes fastest.
Arguments:
- features: bfloat16 [128, 512, 768], P('lat', 'lon'), may hold values from -6 to 6
- upstream: bfloat16 [128, 512, 768], P('lat', 'lon'), may hold values from -6 to 6
- attend_weight: bfloat16 [768, 2304], replicated, may hold values from -0.21875 to 0.21875
- output_weight: bfloat16 [768, 768], replicated, may hold values from -0.21875 to 0.21875
- norm_gain: float32 [768], replicated, may hold values from 0.5 to 1.5
- logit_scale: float32 [24], replicated, may hold values from 0.7 to 3.4
- table_inner: float32 [2, 512], replicated, may hold values from -4 to 4
- table_offset: float32 [512], replicated, may hold values from -0.5 to 0.5
- table_outer: float32 [512, 24], replicated, may hold values from -0.25 to 0.25
- validity: int32 [128, 512], P('lat', 'lon'), may hold values 0 or 1
Outputs:
- input_delta: bfloat16 [128, 512, 768], P('lat', 'lon')
- attend_delta: float32 [768, 2304], P('lon')
- output_delta: float32 [768, 768], P('lon')
- gain_delta: float32 [768], replicated
- scale_delta: float32 [24], replicated
- inner_delta: float32 [2, 512], replicated
- offset_delta: float32 [512], replicated
- outer_delta: float32 [512, 24], replicated
The draws below stay inside these ranges and needn't reach their ends.
Inputs may be any that keep to these rules, and one draw needn't show every extreme that they name: `validity`: 1 marks a valid token.
All inputs are finite; a program needn't handle non-finite values. No bound on the sum of `validity` on one device may be relied on, other than what follows from the above.
Results may differ from the reference program's by a relative error of at most 0.025.
Values may be sent and summed in bfloat16 or wider, within the bound.
No kernel may reach another device: no remote copies, remote signals or barrier semaphores. Data moves between devices by JAX's collectives and lax.ppermute only.
A program may use at most 256 MiB of HBM per device.

```python
import jax
import jax.numpy as jnp
from jax import lax

D = 768
HEADS = 24
HEAD_DIM = 32
TABLE_HIDDEN = 512
WIN = 16
SHIFT = 8
NLAT = 128
NLON = 512


def place_ends(values, own_key, least, largest):
    longest = values.shape.index(max(values.shape))
    spots = []
    for shift in (0, 1):
        where = [jax.random.randint(jax.random.fold_in(own_key, axis), (), 0, length) for axis, length in enumerate(values.shape)]
        where[longest] = (where[longest] + shift) % values.shape[longest]
        spots.append(tuple(where))
    return values.at[spots[0]].set(least).at[spots[1]].set(largest)


def raised(drawn, own_key, source, target, blocks, factor):
    owner, partner = [(jnp.arange(drawn.shape[axis_at]) // (drawn.shape[axis_at] // blocks)).reshape([-1 if axis == axis_at else 1 for axis in range(drawn.ndim)]) for axis_at in (source, target)]
    chosen = jax.random.permutation(own_key, blocks)[partner]
    strong = (owner == chosen) | (owner == (partner + blocks // 2) % blocks)
    return jnp.where(strong, factor * drawn, drawn)


def block_levels(stream_key, shape, cuts, smallest, high):
    def one(dim, parts):
        heights = jax.random.uniform(jax.random.fold_in(jax.random.fold_in(stream_key, 6), dim), (parts,), jnp.float32, smallest / len(cuts), high / len(cuts))
        return jnp.repeat(jnp.exp(heights), shape[dim] // parts).reshape((-1,) + (1,) * (len(shape) - dim - 1))

    gain = one(*cuts[0])
    for cut in cuts[1:]:
        gain = gain * one(*cut)
    return gain


def scatter_about(stream_key, extent, width, reach, split=(), kind=jnp.bfloat16):
    level = block_levels(stream_key, extent, split, -0.22, 0.18) if split else 1.0
    values = jax.random.normal(stream_key, extent, jnp.float32) * width * level
    return jnp.minimum(jnp.maximum(values, -reach), reach).astype(kind)


def noise_with(own_key, dims, width, most, cuts, heavy, held_as=jnp.bfloat16):
    array = width * jax.random.normal(own_key, dims, jnp.float32)
    if cuts:
        array = array * block_levels(own_key, dims, cuts, -0.22, 0.18)
    return jnp.clip(raised(array, jax.random.fold_in(own_key, 3), *heavy), -most, most).astype(held_as)


def setup_inputs(seed: int = 0) -> dict:
    streams_of = jax.random.split(jax.random.key(seed), 11)
    features = noise_with(streams_of[0], (NLAT, NLON, D), 1.0, 6.0, ((0, 8), (1, 32)), (1, 2, 32, 2.75))
    upstream = scatter_about(streams_of[1], (NLAT, NLON, D), 1.0, 6.0, ((0, 8), (1, 32)))
    attend_weight = scatter_about(streams_of[2], (D, 3 * D), D ** -0.5, 0.21875)
    output_weight = scatter_about(streams_of[3], (D, D), D ** -0.5, 0.21875)
    norm_gain = jnp.clip(1.0 + 0.1 * jax.random.normal(streams_of[4], (D,), jnp.float32), 0.5, 1.5)
    logit_scale = jnp.clip(jax.random.uniform(streams_of[5], (HEADS,), jnp.float32, 0.7, 3.4), 0.7, 3.4)
    table_inner = scatter_about(streams_of[6], (2, TABLE_HIDDEN), 2 ** -0.5, 4.0, (), jnp.float32)
    table_offset = jnp.clip(jax.random.uniform(streams_of[7], (TABLE_HIDDEN,), jnp.float32, -0.5, 0.5), -0.5, 0.5)
    table_outer = scatter_about(streams_of[8], (TABLE_HIDDEN, HEADS), TABLE_HIDDEN ** -0.5, 0.25, (), jnp.float32)
    validity = place_ends((jax.random.randint(streams_of[9], (NLAT, NLON), 0, 4) < 3).astype(jnp.int32), jax.random.fold_in(streams_of[9], 1), 0, 1)
    return {"features": features, "upstream": upstream, "attend_weight": attend_weight, "output_weight": output_weight, "norm_gain": norm_gain, "logit_scale": logit_scale, "table_inner": table_inner, "table_offset": table_offset, "table_outer": table_outer, "validity": validity}


exact_mode = lax.Precision.HIGHEST

def offset_coords():
    spread = jnp.arange(2 * WIN - 1, dtype=jnp.float32) - (WIN - 1)
    spread = spread * (8.0 / (WIN - 1))
    spread = jnp.sign(spread) * jnp.log2(1.0 + jnp.abs(spread)) / 3.0
    first_axis = jnp.broadcast_to(spread[:, None], (2 * WIN - 1, 2 * WIN - 1))
    second = jnp.broadcast_to(spread[None, :], (2 * WIN - 1, 2 * WIN - 1))
    return jnp.stack([first_axis, second], -1).reshape(-1, 2)

def table_forward(table_inner, table_offset, table_outer):
    coords = offset_coords()
    before = jnp.dot(coords, table_inner, precision=exact_mode) + table_offset
    hidden = jnp.maximum(before, 0.0)
    logits = jnp.dot(hidden, table_outer, precision=exact_mode)
    return (coords, before, hidden, logits, 16.0 * jax.nn.sigmoid(logits))

def table_backward(grid_delta, coords, before, hidden, logits, table_outer):
    sigmoid_out = jax.nn.sigmoid(logits)
    dlogits = 16.0 * grid_delta * sigmoid_out * (1.0 - sigmoid_out)
    outer_delta = jnp.dot(hidden.T, dlogits, precision=exact_mode)
    dhidden = jnp.dot(dlogits, table_outer.T, precision=exact_mode)
    dhidden = jnp.where(before > 0.0, dhidden, 0.0)
    offset_delta = lax.optimization_barrier(jnp.sum(dhidden, 0))
    inner_delta = jnp.dot(coords.T, dhidden, precision=exact_mode)
    return (inner_delta, offset_delta, outer_delta)

def reference(features, upstream, attend_weight, output_weight, norm_gain, logit_scale, table_inner, table_offset, table_outer, validity):
    rows_total, cols_total, model_width = features.shape
    shifted = jnp.roll(features, (-SHIFT, -SHIFT), (0, 1))
    shifted_up = jnp.roll(upstream, (-SHIFT, -SHIFT), (0, 1))

    def windowed(grid):
        last_dims = grid.shape[2:]
        blocks = grid.reshape((rows_total // WIN, WIN, cols_total // WIN, WIN) + last_dims)
        order = (0, 2, 1, 3) + tuple(range(4, 4 + len(last_dims)))
        return jnp.transpose(blocks, order).reshape((-1, WIN * WIN) + last_dims)
    row_ids = jnp.broadcast_to(jnp.arange(rows_total, dtype=jnp.int32)[:, None], (rows_total, cols_total))
    region = (row_ids >= rows_total - SHIFT).astype(jnp.int32)
    window_tokens = windowed(shifted)
    window_up = windowed(shifted_up)
    window_region = windowed(region)
    window_valid = windowed(validity)
    coords, before, hidden, logits, bias_grid = table_forward(table_inner, table_offset, table_outer)
    positions = jnp.arange(WIN * WIN, dtype=jnp.int32)
    pos_row = positions // WIN
    pos_col = positions % WIN
    index = ((pos_row[:, None] - pos_row[None, :] + WIN - 1) * (2 * WIN - 1) + (pos_col[:, None] - pos_col[None, :] + WIN - 1)).astype(jnp.int32)
    window_bias = jnp.transpose(bias_grid[index], (2, 0, 1))
    scale_factor = jnp.exp(logit_scale)
    diagonal_mask = jnp.eye(WIN * WIN, dtype=bool)
    f32 = jnp.float32
    bf16 = jnp.bfloat16

    def one_window(running, pieces):
        attend_sum, output_sum, gain_sum, scale_sum, bias_sum = running
        tokens, up_tokens, region_ids, valid_ids = pieces
        allowed = ((region_ids[:, None] == region_ids[None, :]) & ((valid_ids[None, :] == 1) | diagonal_mask)).astype(f32)
        projected = jnp.dot(tokens, attend_weight, preferred_element_type=f32)
        queries = projected[:, :model_width].reshape(-1, HEADS, HEAD_DIM)
        key_rows = projected[:, model_width:2 * model_width].reshape(-1, HEADS, HEAD_DIM)
        value_rows = projected[:, 2 * model_width:].reshape(-1, HEADS, HEAD_DIM)
        query_norm = jnp.sqrt(lax.optimization_barrier(jnp.sum(queries * queries, -1, keepdims=True)) + 1.0)
        key_norm = jnp.sqrt(lax.optimization_barrier(jnp.sum(key_rows * key_rows, -1, keepdims=True)) + 1.0)
        query_unit = queries / query_norm
        key_unit = key_rows / key_norm
        query_round = (query_unit * scale_factor[None, :, None]).astype(bf16)
        key_round = key_unit.astype(bf16)
        value_round = value_rows.astype(bf16)
        cosines = jnp.einsum('ihd,jhd->hij', query_round.astype(f32), key_round.astype(f32))
        weights = jnp.exp(cosines + window_bias) * allowed[None]
        softmax_out = weights / lax.optimization_barrier(jnp.sum(weights, -1, keepdims=True))
        softmax_round = softmax_out.astype(bf16)
        heads_out = jnp.einsum('hij,jhd->ihd', softmax_round.astype(f32), value_round.astype(f32))
        heads_out = heads_out.astype(bf16).reshape(-1, model_width)
        mixed_out = jnp.dot(heads_out, output_weight, preferred_element_type=f32)
        centre = lax.optimization_barrier(jnp.mean(mixed_out, -1, keepdims=True))
        variance = lax.optimization_barrier(jnp.mean((mixed_out - centre) ** 2, -1, keepdims=True))
        inverse = 1.0 / jnp.sqrt(variance + 1e-05)
        normed = (mixed_out - centre) * inverse
        up_float = up_tokens.astype(f32)
        dnormed = up_float * norm_gain
        dmixed = (dnormed - lax.optimization_barrier(jnp.mean(dnormed, -1, keepdims=True)) - normed * lax.optimization_barrier(jnp.mean(dnormed * normed, -1, keepdims=True))) * inverse
        dmixed = dmixed.astype(bf16)
        output_sum = output_sum + jnp.dot(heads_out.T, dmixed, preferred_element_type=f32)
        dheads = jnp.dot(dmixed, output_weight.T, preferred_element_type=f32).astype(bf16)
        dheads = dheads.reshape(-1, HEADS, HEAD_DIM)
        dprobs = jnp.einsum('ihd,jhd->hij', dheads.astype(f32), value_round.astype(f32))
        dscores = softmax_out * (dprobs - lax.optimization_barrier(jnp.sum(softmax_out * dprobs, -1, keepdims=True)))
        dscores_round = dscores.astype(bf16)
        value_delta = jnp.einsum('hij,ihd->jhd', softmax_round.astype(f32), dheads.astype(f32))
        query_grad = jnp.einsum('hij,jhd->ihd', dscores_round.astype(f32), key_round.astype(f32))
        query_grad = query_grad * scale_factor[None, :, None]
        key_grad = jnp.einsum('hij,ihd->jhd', dscores_round.astype(f32), query_round.astype(f32))
        query_delta = (query_grad - query_unit * lax.optimization_barrier(jnp.sum(query_unit * query_grad, -1, keepdims=True))) / query_norm
        key_delta = (key_grad - key_unit * lax.optimization_barrier(jnp.sum(key_unit * key_grad, -1, keepdims=True))) / key_norm
        dprojected = jnp.concatenate([query_delta.reshape(-1, model_width), key_delta.reshape(-1, model_width), value_delta.reshape(-1, model_width)], 1).astype(bf16)
        attend_sum = attend_sum + jnp.dot(tokens.T, dprojected, preferred_element_type=f32)
        dtokens = (up_float + jnp.dot(dprojected, attend_weight.T, preferred_element_type=f32)).astype(bf16)
        gain_sum = gain_sum + lax.optimization_barrier(jnp.sum(up_float * normed, 0))
        scale_sum = scale_sum + lax.optimization_barrier(jnp.sum(dscores * cosines, (1, 2)))
        bias_sum = bias_sum + dscores
        return ((attend_sum, output_sum, gain_sum, scale_sum, bias_sum), dtokens)
    start_state = (jnp.zeros((model_width, 3 * model_width), jnp.float32), jnp.zeros((model_width, model_width), jnp.float32), jnp.zeros((model_width,), jnp.float32), jnp.zeros((HEADS,), jnp.float32), jnp.zeros((HEADS, WIN * WIN, WIN * WIN), jnp.float32))
    final_state, dwindows = lax.scan(one_window, start_state, (window_tokens, window_up, window_region, window_valid))
    attend_delta, output_delta, gain_delta, scale_delta, bias_sum = final_state
    dgrid = dwindows.reshape(rows_total // WIN, cols_total // WIN, WIN, WIN, model_width)
    dgrid = jnp.transpose(dgrid, (0, 2, 1, 3, 4)).reshape(rows_total, cols_total, model_width)
    input_delta = jnp.roll(dgrid, (SHIFT, SHIFT), (0, 1))
    grid_delta = jax.ops.segment_sum(jnp.transpose(bias_sum, (1, 2, 0)).reshape(-1, HEADS), index.reshape(-1), num_segments=(2 * WIN - 1) ** 2)
    inner_delta, offset_delta, outer_delta = table_backward(grid_delta, coords, before, hidden, logits, table_outer)
    return (input_delta, attend_delta, output_delta, gain_delta, scale_delta, inner_delta, offset_delta, outer_delta)
```

```python
import functools

import jax
import jax.numpy as jnp
import numpy as np
from jax import lax
from jax.experimental import pallas as pl
from jax.experimental.pallas import tpu as pltpu
from jax.sharding import PartitionSpec as P

D = 768
HEADS = 24
HEAD_DIM = 32
HIDDEN = 512
WIN = 16
SHIFT = 8
AREA = WIN * WIN
QUAD = SHIFT * SHIFT
SLOTS = 1024
PART = 384
BLOCK = 24
BOTH = ("lat", "lon")
NEG = -1e30

f32 = jnp.float32
bf16 = jnp.bfloat16
exact = lax.Precision.HIGHEST

NN = (((1,), (0,)), ((), ()))
NT = (((1,), (1,)), ((), ()))
TN = (((0,), (0,)), ((), ()))


def mm(a, b, dims=NN, precision=None):
    return lax.dot_general(a, b, dims, precision=precision, preferred_element_type=f32)


def slot_coords():
    slot = lax.broadcasted_iota(jnp.int32, (SLOTS, 128), 0)
    row = (slot // 32) % 16 * 2 + slot // 512
    out = []
    for index in (row, slot % 32):
        spread = (index - (WIN - 1)).astype(f32) * (8.0 / (WIN - 1))
        size = jnp.log(1.0 + jnp.abs(spread)) * (1.0 / (3.0 * np.log(2.0)))
        out.append(jnp.concatenate([jnp.where(spread < 0.0, -size, size)] * 4, 1))
    return out


def hidden_of(inner_ref, offset_ref):
    first, second = slot_coords()
    before = first * inner_ref[0:1, :] + second * inner_ref[1:2, :] + offset_ref[...]
    return first, second, before, jnp.maximum(before, 0.0)


def fetch(pairs, sems, first=0):
    copies = [
        pltpu.make_async_copy(source, target, sems.at[first + n]) for n, (source, target) in enumerate(pairs)
    ]
    for copy in copies:
        copy.start()
    return copies


def cut_kernel(features_hbm, upstream_hbm, o00, o01, o10, o11, features_ref, upstream_ref, sems):
    outs = (o00, o01, o10, o11)
    for copy in fetch(((features_hbm, features_ref), (upstream_hbm, upstream_ref)), sems):
        copy.wait()
    feats = features_ref[...].astype(f32)
    ups = upstream_ref[...].astype(f32)
    for (r, c), out in zip(((8, 8), (8, 0), (0, 8), (0, 0)), outs):
        out[0:QUAD, :] = feats[r : r + 8, c : c + 8].reshape(QUAD, D).astype(bf16)
        out[QUAD:, :] = ups[r : r + 8, c : c + 8].reshape(QUAD, D).astype(bf16)


def bias_kernel(
    last_ref, log_ref, inner_hbm, offset_hbm, outer_hbm, valid_hbm,
    table_ref, mask_ref, factor_ref,
    inner_ref, offset_ref, outer_ref, valid_ref, rows_ref, in_sems,
):
    for copy in fetch(
        (
            (inner_hbm, inner_ref),
            (offset_hbm, offset_ref),
            (outer_hbm, outer_ref),
            (valid_hbm, valid_ref),
        ),
        in_sems,
    ):
        copy.wait()
    hidden = hidden_of(inner_ref, offset_ref)[3]
    logits = mm(outer_ref[...], hidden, NT, exact)
    grid = 16.0 * jax.nn.sigmoid(logits)
    even = grid[:, :512]
    odd = grid[:, 512:]
    lane = lax.broadcasted_iota(jnp.int32, (HEADS, 512), 1)
    first = (lane % 32) < 16
    for cj in range(WIN):
        rows_ref[cj] = jnp.where(
            first,
            pltpu.roll(even, (512 - 15 + cj) % 512, 1),
            pltpu.roll(odd, (1 + cj) % 512, 1),
        )
    valid = valid_ref[...].astype(f32).T
    split = last_ref[0] == 1
    cj = lax.broadcasted_iota(jnp.int32, (WIN, AREA), 0)
    query = lax.broadcasted_iota(jnp.int32, (WIN, AREA), 1)
    for rj in range(WIN):
        same = jnp.logical_or((query >= AREA // 2) == (rj >= WIN // 2), jnp.logical_not(split))
        seen = jnp.logical_or(valid[:, rj : rj + 1] == 1.0, rj * WIN + cj == query)
        mask_ref[rj * WIN : (rj + 1) * WIN, :] = jnp.where(jnp.logical_and(same, seen), 0.0, NEG)

    for head in range(HEADS):
        factor_ref[head] = jnp.exp(jnp.full((1, AREA), log_ref[head], f32))
        table_ref[head] = rows_ref[:, head : head + 1, :].reshape(WIN, 512)


def window_kernel(
    core_ref, factor_ref, table_ref, mask_ref, q00, q01, q10, q11, gain_hbm, weight_hbm, out_weight_hbm,
    send_ref, keep_ref, d00, d01, d10, d11, gain_out, scale_out, table_out,
    grid3, up, tokt, projt, exps, inv, hot, doutt, weight_ref, out_weight_ref, gain_ref, sems,
):
    weight_copies = [
        pltpu.make_async_copy(
            weight_hbm.at[:, part * PART : (part + 1) * PART],
            weight_ref.at[:, part * PART : (part + 1) * PART],
            sems.at[part],
        )
        for part in range(6)
    ]
    out_weight_copy = pltpu.make_async_copy(out_weight_hbm, out_weight_ref, sems.at[6])
    gain_copy = pltpu.make_async_copy(gain_hbm, gain_ref, sems.at[7])
    for copy in weight_copies:
        copy.start()
    gain_copy.start()
    out_weight_copy.start()

    places = ((0, 0), (0, 8), (8, 0), (8, 8))
    quads = (q00, q01, q10, q11)

    def assemble(rows):
        for (r, c), part in zip(places, quads):
            grid3[r : r + 8, c : c + 8, :] = part[rows, :].astype(f32).reshape(8, 8, D)
        return grid3[...].reshape(AREA, D)

    def rows_of(source, core):
        pieces = []
        for hi in range(2):
            for z in range(8):
                at = pl.multiple_of((hi * 16 + z * 2 + core) * BLOCK, 8)
                pieces.append(source[pl.ds(at, BLOCK), :])
        return jnp.concatenate(pieces, 0).astype(bf16)

    mine = core_ref[0]
    up[...] = assemble(slice(QUAD, 2 * QUAD))
    tokens32 = assemble(slice(0, QUAD))
    tokens = tokens32.astype(bf16)
    tokt[...] = tokens32.T
    for part in range(6):
        cols = slice(part * PART, (part + 1) * PART)
        weight_copies[part].wait()
        projt[cols, :] = mm(tokens, weight_ref[:, cols]).T
    keep_ref[0:384, :] = rows_of(tokt, mine)
    send_ref[0:384, :] = rows_of(tokt, 1 - mine)

    def head_inputs(head):
        at = pl.multiple_of(head * HEAD_DIM, HEAD_DIM)
        q = projt[pl.ds(at, HEAD_DIM), :]
        k = projt[pl.ds(D + at, HEAD_DIM), :]
        v = projt[pl.ds(2 * D + at, HEAD_DIM), :]
        q_inv = lax.rsqrt(jnp.sum(q * q, 0, keepdims=True) + 1.0)
        k_inv = lax.rsqrt(jnp.sum(k * k, 0, keepdims=True) + 1.0)
        q_unit = q * q_inv
        k_unit = k * k_inv
        factor = factor_ref[head]
        return at, q_unit, q_inv, (q_unit * factor).astype(bf16), k_unit, k_inv, k_unit.astype(bf16), v, factor

    extra = lax.broadcasted_iota(jnp.int32, (16, AREA), 0)

    def forward_head(head, carry):
        at, _, _, q_round, _, _, k_round, v, _ = head_inputs(head)
        scores = mm(k_round, q_round, TN)
        table = table_ref[head]
        slabs = [None] * WIN
        for b in range(8):
            turned = table if b == 0 else pltpu.roll(table, 512 - 16 * b, 1)
            for a in range(2):
                rj = 15 - (8 * a + b)
                rows = slice(rj * 16, rj * 16 + 16)
                slabs[rj] = jnp.exp(
                    scores[rows, :] + (turned[:, 128 * a : 128 * a + 256] + mask_ref[rows, :])
                ).astype(bf16)
        weights = jnp.concatenate(slabs, 0)
        exps[head] = weights
        values = jnp.concatenate([v, jnp.where(extra == 0, 1.0, 0.0)], 0).astype(bf16)
        mixed = mm(values, weights)
        inverse = 1.0 / mixed[HEAD_DIM : HEAD_DIM + 1, :]
        inv[head] = inverse
        hot[pl.ds(at, HEAD_DIM), :] = mixed[:HEAD_DIM, :] * inverse
        return carry

    lax.fori_loop(0, HEADS, forward_head, 0, unroll=12)

    keep_ref[384:768, :] = rows_of(hot, mine)
    send_ref[384:768, :] = rows_of(hot, 1 - mine)
    out_weight_copy.wait()
    gain_copy.wait()
    heads_out = hot[...].T.astype(bf16)
    mixed_out = mm(heads_out, out_weight_ref[...])
    centre = jnp.mean(mixed_out, -1, keepdims=True)
    shifted = mixed_out - centre
    inverse = lax.rsqrt(jnp.mean(shifted * shifted, -1, keepdims=True) + 1e-05)
    normed = shifted * inverse
    up_now = up[...]
    gain_out[...] = jnp.sum(up_now * normed, 0, keepdims=True)
    dnormed = up_now * gain_ref[...].reshape(1, D)
    dmixed = (
        dnormed
        - jnp.mean(dnormed, -1, keepdims=True)
        - normed * jnp.mean(dnormed * normed, -1, keepdims=True)
    ) * inverse
    dmixed = dmixed.astype(bf16)
    for part in range(3):
        send_ref[3072 + part * AREA : 3072 + (part + 1) * AREA, :] = dmixed[:, part * AREA : (part + 1) * AREA]
    doutt[...] = mm(out_weight_ref[...], dmixed, NT).astype(bf16)

    def backward_head(head, carry):
        at, q_unit, q_inv, q_round, k_unit, k_inv, k_round, v, factor = head_inputs(head)
        weights = exps[head]
        inverse = inv[head]
        dout = (doutt[pl.ds(at, HEAD_DIM), :].astype(f32) * inverse).astype(bf16).astype(f32)
        delta = jnp.sum(dout * hot[pl.ds(at, HEAD_DIM), :], 0, keepdims=True)
        high = delta.astype(bf16).astype(f32)
        tail = jnp.where(extra == 0, high, jnp.where(extra == 1, delta - high, 0.0))
        dout_more = jnp.concatenate([dout, tail], 0).astype(bf16)
        values = jnp.concatenate([v, jnp.where(extra < 2, -1.0, 0.0)], 0).astype(bf16)
        dscores = weights.astype(f32) * mm(values, dout_more, TN)
        dround = dscores.astype(bf16)
        dvalue = mm(dout.astype(bf16), weights, NT)
        dquery = mm(k_round, dround)
        dkey = mm(q_round, dround, NT)
        scale_out[pl.ds(head, 1), :] = jnp.sum(dscores * mm(k_round, q_round, TN), 0, keepdims=True)
        dquery = dquery * factor
        dquery = (dquery - q_unit * jnp.sum(q_unit * dquery, 0, keepdims=True)) * q_inv
        dkey = (dkey - k_unit * jnp.sum(k_unit * dkey, 0, keepdims=True)) * k_inv
        send_ref[pl.ds(768 + at, HEAD_DIM), :] = dquery.astype(bf16)
        send_ref[pl.ds(768 + D + at, HEAD_DIM), :] = dkey.astype(bf16)
        send_ref[pl.ds(768 + 2 * D + at, HEAD_DIM), :] = dvalue.astype(bf16)
        total = None
        for b in range(8):
            near = dscores[(15 - b) * 16 : (15 - b) * 16 + 16, :]
            far = dscores[(7 - b) * 16 : (7 - b) * 16 + 16, :]
            wide = jnp.concatenate(
                [near[:, :128], near[:, 128:] + far[:, :128], far[:, 128:], jnp.zeros((16, 128), f32)], 1
            )
            if b:
                wide = pltpu.roll(wide, 16 * b, 1)
            total = wide if total is None else total + wide
        table_out[head] = total
        return carry

    lax.fori_loop(0, HEADS, backward_head, 0, unroll=24)

    dtokens = up[...] + mm(weight_ref[...], send_ref[768:3072, :]).T
    grid3[...] = dtokens.reshape(WIN, WIN, D)
    for (r, c), part in zip(places, (d00, d01, d10, d11)):
        part[...] = grid3[r : r + 8, c : c + 8, :].reshape(QUAD, D).astype(bf16)


def table_kernel(
    inner_hbm, offset_hbm, outer_hbm, table_ref, gain_ref, scale_ref,
    pack_ref,
    inner_ref, offset_ref, outer_ref, rows_ref, work_ref, sems,
):
    for copy in fetch(((inner_hbm, inner_ref), (offset_hbm, offset_ref), (outer_hbm, outer_ref)), sems):
        copy.wait()
    first_coord, second_coord, before, hidden = hidden_of(inner_ref, offset_ref)
    logits = mm(outer_ref[...], hidden, NT, exact)
    sig = jax.nn.sigmoid(logits)
    lane = lax.broadcasted_iota(jnp.int32, (HEADS, 512), 1)
    first = (lane % 32) < 16
    for head in range(HEADS):
        rows_ref[:, head : head + 1, :] = table_ref[head].reshape(WIN, 1, 512)
    even = jnp.zeros((HEADS, 512), f32)
    odd = jnp.zeros((HEADS, 512), f32)
    for cj in range(WIN):
        row = rows_ref[cj]
        even = even + pltpu.roll(jnp.where(first, row, 0.0), 15 - cj, 1)
        odd = odd + pltpu.roll(jnp.where(first, 0.0, row), (512 - 1 - cj) % 512, 1)
    dgrid = jnp.concatenate([even, odd], 1)
    dlogits = 16.0 * dgrid * sig * (1.0 - sig)
    outer = mm(dlogits, hidden, NN, exact)
    dhidden = mm(dlogits, outer_ref[...], TN, exact)
    dhidden = jnp.where(before > 0.0, dhidden, 0.0)
    scale = jnp.sum(scale_ref[...], -1, keepdims=True)
    where_row = lax.broadcasted_iota(jnp.int32, (HEADS, PART), 0)
    where_lane = lax.broadcasted_iota(jnp.int32, (HEADS, PART), 1)
    first_inner = jnp.sum(first_coord * dhidden, 0, keepdims=True)
    second_inner = jnp.sum(second_coord * dhidden, 0, keepdims=True)
    offset = jnp.sum(dhidden, 0, keepdims=True)
    work_ref[0:HEADS, :] = outer[:, :PART]
    for head in range(HEADS):
        place = (head % 3) * 128
        work_ref[24 + head // 3 : 25 + head // 3, place : place + 128] = outer[head : head + 1, PART:]
    work_ref[32:33, :] = first_inner[:, :PART]
    work_ref[33:34, :] = second_inner[:, :PART]
    work_ref[34:35, :] = jnp.concatenate([first_inner[:, PART:], second_inner[:, PART:], offset[:, PART:]], 1)
    work_ref[35:36, :] = offset[:, :PART]
    work_ref[36:37, :] = gain_ref[:, :PART]
    work_ref[37:38, :] = gain_ref[:, PART:]
    work_ref[38:39, :] = jnp.sum(jnp.where(where_row == where_lane, scale, 0.0), 0, keepdims=True)
    work_ref[39:64, :] = jnp.zeros((25, PART), f32)
    pack_ref[...] = work_ref[...].astype(bf16)


def grads_kernel(keep_ref, send_ref, got_ref, pack_ref, got_pack_ref, out_ref):
    pack = pack_ref[...].astype(f32) + got_pack_ref[...].astype(f32)
    for part in range(8):
        for hi in range(2):
            total = None
            for own, source in ((keep_ref, send_ref), (got_ref, got_ref)):
                base = hi * 192 + (384 if part >= 6 else 0)
                rows = own[base : base + 192, :]
                if part < 6:
                    piece = mm(rows, source[768 + part * PART : 768 + (part + 1) * PART, :], NT)
                else:
                    first = 3072 if part == 6 else 3072 + AREA
                    halves = [
                        mm(rows, source[first + n * AREA : first + (n + 1) * AREA, :]) for n in range(2)
                    ]
                    if part == 6:
                        piece = jnp.concatenate([halves[0], halves[1][:, :128]], 1)
                    else:
                        piece = jnp.concatenate([halves[0][:, 128:], halves[1]], 1)
                total = piece if total is None else total + piece
            out_ref[hi * 8 + part] = jnp.concatenate([total, pack[part * 8 : part * 8 + 8]], 0).astype(bf16)


def plane_kernel(in_ref, out_ref):
    total = in_ref[0].astype(f32)
    for n in range(1, 16):
        total = total + in_ref[n].astype(f32)
    for z in range(8):
        out_ref[z] = jnp.concatenate([total[z * BLOCK : (z + 1) * BLOCK], total[192:200]], 0).astype(bf16)


def column_kernel(in_ref, out_ref):
    total = in_ref[0].astype(f32)
    for n in range(1, 8):
        total = total + in_ref[n].astype(f32)
    both = total.astype(bf16)
    for n in range(8):
        out_ref[n] = both


def finish_kernel(in_ref, attend_ref, output_ref, gain_ref, scale_ref, inner_ref, offset_ref, outer_ref, work_ref):
    for part in range(8):
        piece = in_ref[part].astype(f32)
        if part < 6:
            attend_ref[:, part * PART : (part + 1) * PART] = piece[:BLOCK]
        else:
            output_ref[:, (part - 6) * PART : (part - 5) * PART] = piece[:BLOCK]
        work_ref[part * 8 : part * 8 + 8, :] = piece[24:32]
    tails = [
        work_ref[24 + head // 3 : 25 + head // 3, (head % 3) * 128 : (head % 3) * 128 + 128] for head in range(HEADS)
    ]
    outer = jnp.concatenate([work_ref[0:HEADS, :], jnp.concatenate(tails, 0)], 1)
    outer_ref[...] = outer
    inner_ref[0:1, :PART] = work_ref[32:33, :]
    inner_ref[1:2, :PART] = work_ref[33:34, :]
    inner_ref[0:1, PART:] = work_ref[34:35, 0:128]
    inner_ref[1:2, PART:] = work_ref[34:35, 128:256]
    offset_ref[...] = jnp.concatenate([work_ref[35:36, :], work_ref[34:35, 256:]], 1).reshape(HIDDEN)
    gain_ref[...] = jnp.concatenate([work_ref[36:37, :], work_ref[37:38, :]], 1).reshape(D)
    scale_ref[...] = work_ref[38:39, :].reshape(PART)[:HEADS]


def vmem(count):
    return [pl.BlockSpec(memory_space=pltpu.VMEM)] * count


HBM = pl.BlockSpec(memory_space=pltpu.MemorySpace.HBM)
SMEM = pl.BlockSpec(memory_space=pltpu.SMEM)


def params(mib):
    return pltpu.CompilerParams(vmem_limit_bytes=mib * 1024 * 1024)


def cost(micros):
    return pl.CostEstimate(flops=int(micros * 1.15e9), bytes_accessed=0, transcendentals=0)


def place_of(lat, hi, z, core):
    return lat * 32 + hi * 16 + z * 2 + core


def shift_pairs(lat_step, lon_step):
    return [
        (lat * 32 + lon, ((lat + lat_step) % 8) * 32 + (lon + lon_step) % 32)
        for lat in range(8)
        for lon in range(32)
    ]


PLANE = [[place_of(lat, hi, z, core) for hi in range(2) for lat in range(8)] for z in range(8) for core in range(2)]
COLUMN = [[place_of(lat, hi, z, core) for z in range(8)] for lat in range(8) for hi in range(2) for core in range(2)]
LATS = [[place_of(lat, hi, z, core) for lat in range(8)] for hi in range(2) for z in range(8) for core in range(2)]
CORES = [
    (place_of(lat, hi, z, core), place_of(lat, hi, z, 1 - core))
    for lat in range(8)
    for hi in range(2)
    for z in range(8)
    for core in range(2)
]


def exchange(value, groups):
    return lax.all_to_all(value, BOTH, 0, 0, axis_index_groups=groups, tiled=True)


def per_device(
    features, upstream, attend_weight, output_weight, norm_gain, logit_scale,
    table_inner, table_offset, table_outer, validity,
):
    steps = ((0, 0), (0, 1), (1, 0), (1, 1))
    both = pl.pallas_call(
        cut_kernel,
        out_shape=(jax.ShapeDtypeStruct((2 * QUAD, D), bf16),) * 4,
        in_specs=[HBM] * 2,
        out_specs=tuple(vmem(4)),
        scratch_shapes=[pltpu.VMEM((WIN, WIN, D), bf16)] * 2 + [pltpu.SemaphoreType.DMA((2,))],
        compiler_params=params(16),
        cost_estimate=cost(2),
        name="cut",
    )(features, upstream)
    moved = [
        value if step == (0, 0) else lax.ppermute(value, BOTH, shift_pairs(-step[0], -step[1]))
        for step, value in zip(steps, both)
    ]

    outer_t = table_outer.T
    offset_row = table_offset.reshape(1, HIDDEN)
    last = (lax.axis_index("lat") == lax.axis_size("lat") - 1).astype(jnp.int32).reshape(1)
    core = (lax.axis_index("lon") % 2).astype(jnp.int32).reshape(1)
    bias, mask, factor = pl.pallas_call(
        bias_kernel,
        out_shape=(
            jax.ShapeDtypeStruct((HEADS, WIN, 512), f32),
            jax.ShapeDtypeStruct((AREA, AREA), f32),
            jax.ShapeDtypeStruct((HEADS, 1, AREA), f32),
        ),
        in_specs=[SMEM] * 2 + [HBM] * 4,
        out_specs=tuple(vmem(3)),
        scratch_shapes=[
            pltpu.VMEM((2, HIDDEN), f32),
            pltpu.VMEM((1, HIDDEN), f32),
            pltpu.VMEM((HEADS, HIDDEN), f32),
            pltpu.VMEM((WIN, WIN), jnp.int32),
            pltpu.VMEM((WIN, HEADS, 512), f32),
            pltpu.SemaphoreType.DMA((4,)),
        ],
        compiler_params=params(16),
        cost_estimate=cost(30),
        name="bias",
    )(last, logit_scale, table_inner, offset_row, outer_t, validity)

    quad_shape = jax.ShapeDtypeStruct((QUAD, D), bf16)
    send, keep, *dquads, gain_part, scale_part, table_part = pl.pallas_call(
        window_kernel,
        out_shape=(
            jax.ShapeDtypeStruct((3840, AREA), bf16),
            jax.ShapeDtypeStruct((768, AREA), bf16),
            quad_shape,
            quad_shape,
            quad_shape,
            quad_shape,
            jax.ShapeDtypeStruct((1, D), f32),
            jax.ShapeDtypeStruct((HEADS, AREA), f32),
            jax.ShapeDtypeStruct((HEADS, WIN, 512), f32),
        ),
        in_specs=[SMEM] + vmem(7) + [HBM] * 3,
        out_specs=tuple(vmem(9)),
        scratch_shapes=[
            pltpu.VMEM((WIN, WIN, D), f32),
            pltpu.VMEM((AREA, D), f32),
            pltpu.VMEM((D, AREA), f32),
            pltpu.VMEM((3 * D, AREA), f32),
            pltpu.VMEM((HEADS, AREA, AREA), bf16),
            pltpu.VMEM((HEADS, 1, AREA), f32),
            pltpu.VMEM((D, AREA), f32),
            pltpu.VMEM((D, AREA), bf16),
            pltpu.VMEM((D, 3 * D), bf16),
            pltpu.VMEM((D, D), bf16),
            pltpu.VMEM((D,), f32),
            pltpu.SemaphoreType.DMA((8,)),
        ],
        compiler_params=params(36),
        cost_estimate=cost(17),
        name="window",
    )(core, factor, bias, mask, *moved, norm_gain, attend_weight, output_weight)

    got = lax.ppermute(send, BOTH, CORES)
    pack = pl.pallas_call(
        table_kernel,
        out_shape=jax.ShapeDtypeStruct((64, PART), bf16),
        in_specs=[HBM] * 3 + vmem(3),
        out_specs=vmem(1)[0],
        scratch_shapes=[
            pltpu.VMEM((2, HIDDEN), f32),
            pltpu.VMEM((1, HIDDEN), f32),
            pltpu.VMEM((HEADS, HIDDEN), f32),
            pltpu.VMEM((WIN, HEADS, 512), f32),
            pltpu.VMEM((64, PART), f32),
            pltpu.SemaphoreType.DMA((3,)),
        ],
        compiler_params=params(16),
        cost_estimate=cost(5),
        name="table",
    )(table_inner, offset_row, outer_t, table_part, gain_part, scale_part)
    got_pack = lax.ppermute(pack, BOTH, CORES)
    grads = pl.pallas_call(
        grads_kernel,
        out_shape=jax.ShapeDtypeStruct((16, 200, PART), bf16),
        in_specs=vmem(5),
        out_specs=vmem(1)[0],
        compiler_params=params(24),
        cost_estimate=cost(2),
        name="grads",
    )(keep, send, got, pack, got_pack)
    plane = pl.pallas_call(
        plane_kernel,
        out_shape=jax.ShapeDtypeStruct((8, 32, PART), bf16),
        in_specs=vmem(1),
        out_specs=vmem(1)[0],
        compiler_params=params(16),
        cost_estimate=cost(1),
        name="plane",
    )(exchange(grads, PLANE))
    late = lax.optimization_barrier((plane, *dquads))
    plane, dquads = late[0], late[1:]
    back = [
        value if step == (0, 0) else lax.ppermute(value, BOTH, shift_pairs(*step))
        for step, value in zip(steps, dquads)
    ]
    held = lax.optimization_barrier((exchange(plane, COLUMN), *back))
    column, back = held[0], held[1:]
    column = pl.pallas_call(
        column_kernel,
        out_shape=jax.ShapeDtypeStruct((8, 32, PART), bf16),
        in_specs=vmem(1),
        out_specs=vmem(1)[0],
        compiler_params=params(16),
        cost_estimate=cost(1),
        name="column",
    )(column)

    back = [value.reshape(SHIFT, SHIFT, D) for value in back]
    input_delta = jnp.concatenate(
        [jnp.concatenate([back[3], back[2]], 1), jnp.concatenate([back[1], back[0]], 1)], 0
    )

    attend_delta, output_delta, gain, scale, inner, offset, outer = pl.pallas_call(
        finish_kernel,
        out_shape=(
            jax.ShapeDtypeStruct((BLOCK, 3 * D), f32),
            jax.ShapeDtypeStruct((BLOCK, D), f32),
            jax.ShapeDtypeStruct((D,), f32),
            jax.ShapeDtypeStruct((HEADS,), f32),
            jax.ShapeDtypeStruct((2, HIDDEN), f32),
            jax.ShapeDtypeStruct((HIDDEN,), f32),
            jax.ShapeDtypeStruct((HEADS, HIDDEN), f32),
        ),
        in_specs=vmem(1),
        out_specs=tuple(vmem(7)),
        scratch_shapes=[pltpu.VMEM((64, PART), f32)],
        compiler_params=params(16),
        cost_estimate=cost(1),
        name="finish",
    )(exchange(column, LATS))
    return (
        input_delta,
        attend_delta,
        output_delta,
        gain,
        scale,
        inner,
        offset,
        outer.T,
    )


def solution(mesh):
    in_specs = (
        P("lat", "lon", None),
        P("lat", "lon", None),
        P(),
        P(),
        P(),
        P(),
        P(),
        P(),
        P(),
        P("lat", "lon"),
    )
    out_specs = (P("lat", "lon", None), P("lon", None), P("lon", None), P(), P(), P(), P(), P())
    return jax.shard_map(
        per_device, mesh=mesh, in_specs=in_specs, out_specs=out_specs, check_vma=False
    )
```

```python
import functools

import jax
import jax.numpy as jnp
import numpy as np
from jax import lax
from jax.experimental import pallas as pl
from jax.experimental.pallas import tpu as pltpu
from jax.sharding import PartitionSpec as P

D = 768
HEADS = 24
HEAD_DIM = 32
HIDDEN = 512
WIN = 16
SHIFT = 8
AREA = WIN * WIN
QUAD = SHIFT * SHIFT
SLOTS = 1024
PART = 384
BLOCK = 24
BOTH = ("lat", "lon")
NEG = -1e30

f32 = jnp.float32
bf16 = jnp.bfloat16
exact = lax.Precision.HIGHEST

NN = (((1,), (0,)), ((), ()))
NT = (((1,), (1,)), ((), ()))
TN = (((0,), (0,)), ((), ()))


def mm(a, b, dims=NN, precision=None):
    return lax.dot_general(a, b, dims, precision=precision, preferred_element_type=f32)


def slot_coords():
    slot = lax.broadcasted_iota(jnp.int32, (SLOTS, 128), 0)
    row = (slot // 32) % 16 * 2 + slot // 512
    out = []
    for index in (row, slot % 32):
        spread = (index - (WIN - 1)).astype(f32) * (8.0 / (WIN - 1))
        size = jnp.log(1.0 + jnp.abs(spread)) * (1.0 / (3.0 * np.log(2.0)))
        out.append(jnp.concatenate([jnp.where(spread < 0.0, -size, size)] * 4, 1))
    return out


def hidden_of(inner_ref, offset_ref):
    first, second = slot_coords()
    return jnp.maximum(first * inner_ref[0:1, :] + second * inner_ref[1:2, :] + offset_ref[...], 0.0)


def fetch(pairs, sems, first=0):
    copies = [
        pltpu.make_async_copy(source, target, sems.at[first + n]) for n, (source, target) in enumerate(pairs)
    ]
    for copy in copies:
        copy.start()
    return copies


def cut_kernel(features_hbm, upstream_hbm, o00, o01, o10, o11, features_ref, upstream_ref, sems):
    outs = (o00, o01, o10, o11)
    for copy in fetch(((features_hbm, features_ref), (upstream_hbm, upstream_ref)), sems):
        copy.wait()
    feats = features_ref[...].astype(f32)
    ups = upstream_ref[...].astype(f32)
    for (r, c), out in zip(((8, 8), (8, 0), (0, 8), (0, 0)), outs):
        out[0:QUAD, :] = feats[r : r + 8, c : c + 8].reshape(QUAD, D).astype(bf16)
        out[QUAD:, :] = ups[r : r + 8, c : c + 8].reshape(QUAD, D).astype(bf16)


def bias_kernel(
    last_ref, log_ref, inner_ref, offset_ref, outer_ref, valid_ref, gain_ref,
    table_ref, mask_ref, factor_ref, hidden_ref, slope_ref, gain_out, rows_ref,
):
    gain_out[...] = gain_ref[...].reshape(1, D)
    hidden = hidden_of(inner_ref, offset_ref)
    hidden_ref[...] = hidden
    sig = jax.nn.sigmoid(mm(outer_ref[...], hidden, NT, exact))
    grid = 16.0 * sig
    slope_ref[...] = grid * (1.0 - sig)
    even = grid[:, :512]
    odd = grid[:, 512:]
    lane = lax.broadcasted_iota(jnp.int32, (HEADS, 512), 1)
    first = (lane % 32) < 16
    for cj in range(WIN):
        rows_ref[cj] = jnp.where(
            first,
            pltpu.roll(even, (512 - 15 + cj) % 512, 1),
            pltpu.roll(odd, (1 + cj) % 512, 1),
        )
    valid = valid_ref[...].astype(f32).T
    split = last_ref[0] == 1
    cj = lax.broadcasted_iota(jnp.int32, (WIN, AREA), 0)
    query = lax.broadcasted_iota(jnp.int32, (WIN, AREA), 1)
    for rj in range(WIN):
        same = jnp.logical_or((query >= AREA // 2) == (rj >= WIN // 2), jnp.logical_not(split))
        seen = jnp.logical_or(valid[:, rj : rj + 1] == 1.0, rj * WIN + cj == query)
        mask_ref[rj * WIN : (rj + 1) * WIN, :] = jnp.where(jnp.logical_and(same, seen), 0.0, NEG)

    for head in range(HEADS):
        factor_ref[head] = jnp.exp(jnp.full((1, AREA), log_ref[head], f32))
        table_ref[head] = rows_ref[:, head : head + 1, :].reshape(WIN, 512)


def window_kernel(
    core_ref, factor_ref, table_ref, mask_ref, q00, q01, q10, q11, gain_ref, weight_ref, out_weight_ref,
    send_ref, keep_ref, d00, d01, d10, d11, gain_out, scale_out, table_out,
    grid3, up, tokt, projt, exps, inv, hot, doutt, means,
):
    places = ((0, 0), (0, 8), (8, 0), (8, 8))
    quads = (q00, q01, q10, q11)

    def assemble(rows):
        for (r, c), part in zip(places, quads):
            grid3[r : r + 8, c : c + 8, :] = part[rows, :].astype(f32).reshape(8, 8, D)
        return grid3[...].reshape(AREA, D)

    def rows_of(source, core):
        pieces = []
        for hi in range(2):
            for z in range(8):
                at = pl.multiple_of((hi * 16 + z * 2 + core) * BLOCK, 8)
                pieces.append(source[pl.ds(at, BLOCK), :])
        return jnp.concatenate(pieces, 0).astype(bf16)

    mine = core_ref[0]
    up[...] = assemble(slice(QUAD, 2 * QUAD))
    tokens32 = assemble(slice(0, QUAD))
    tokens = tokens32.astype(bf16)
    tokt[...] = tokens32.T
    for part in range(6):
        cols = slice(part * PART, (part + 1) * PART)
        projt[cols, :] = mm(tokens, weight_ref[:, cols]).T
    keep_ref[0:384, :] = rows_of(tokt, mine)
    send_ref[0:384, :] = rows_of(tokt, 1 - mine)

    def head_inputs(head):
        at = pl.multiple_of(head * HEAD_DIM, HEAD_DIM)
        q = projt[pl.ds(at, HEAD_DIM), :]
        k = projt[pl.ds(D + at, HEAD_DIM), :]
        v = projt[pl.ds(2 * D + at, HEAD_DIM), :]
        q_inv = lax.rsqrt(jnp.sum(q * q, 0, keepdims=True) + 1.0)
        k_inv = lax.rsqrt(jnp.sum(k * k, 0, keepdims=True) + 1.0)
        q_unit = q * q_inv
        k_unit = k * k_inv
        factor = factor_ref[head]
        return at, q_unit, q_inv, (q_unit * factor).astype(bf16), k_unit, k_inv, k_unit.astype(bf16), v, factor

    extra = lax.broadcasted_iota(jnp.int32, (16, AREA), 0)

    def forward_head(head, carry):
        at, _, _, q_round, _, _, k_round, v, _ = head_inputs(head)
        scores = mm(k_round, q_round, TN)
        table = table_ref[head]
        slabs = [None] * WIN
        for b in range(8):
            turned = table if b == 0 else pltpu.roll(table, 512 - 16 * b, 1)
            for a in range(2):
                rj = 15 - (8 * a + b)
                rows = slice(rj * 16, rj * 16 + 16)
                slabs[rj] = jnp.exp(
                    scores[rows, :] + (turned[:, 128 * a : 128 * a + 256] + mask_ref[rows, :])
                ).astype(bf16)
        weights = jnp.concatenate(slabs, 0)
        exps[head] = weights
        values = jnp.concatenate([v, jnp.where(extra == 0, 1.0, 0.0)], 0).astype(bf16)
        mixed = mm(jnp.concatenate([values, k_round], 0), weights)
        inverse = 1.0 / mixed[HEAD_DIM : HEAD_DIM + 1, :]
        inv[head] = inverse
        means[head] = jnp.sum(q_round.astype(f32) * mixed[48:, :], 0, keepdims=True) * inverse
        hot[pl.ds(at, HEAD_DIM), :] = mixed[:HEAD_DIM, :] * inverse
        return carry

    lax.fori_loop(0, HEADS, forward_head, 0, unroll=12)

    keep_ref[384:768, :] = rows_of(hot, mine)
    send_ref[384:768, :] = rows_of(hot, 1 - mine)
    heads_out = hot[...].T.astype(bf16)
    mixed_out = mm(heads_out, out_weight_ref[...])
    centre = jnp.mean(mixed_out, -1, keepdims=True)
    shifted = mixed_out - centre
    inverse = lax.rsqrt(jnp.mean(shifted * shifted, -1, keepdims=True) + 1e-05)
    normed = shifted * inverse
    up_now = up[...]
    gain_out[...] = jnp.sum(up_now * normed, 0, keepdims=True)
    dnormed = up_now * gain_ref[...]
    dmixed = (
        dnormed
        - jnp.mean(dnormed, -1, keepdims=True)
        - normed * jnp.mean(dnormed * normed, -1, keepdims=True)
    ) * inverse
    dmixed = dmixed.astype(bf16)
    for part in range(3):
        send_ref[3072 + part * AREA : 3072 + (part + 1) * AREA, :] = dmixed[:, part * AREA : (part + 1) * AREA]
    doutt[...] = mm(out_weight_ref[...], dmixed, NT).astype(bf16)

    def backward_head(head, carry):
        at, q_unit, q_inv, q_round, k_unit, k_inv, k_round, v, factor = head_inputs(head)
        weights = exps[head]
        inverse = inv[head]
        dout = (doutt[pl.ds(at, HEAD_DIM), :].astype(f32) * inverse).astype(bf16).astype(f32)
        delta = jnp.sum(dout * hot[pl.ds(at, HEAD_DIM), :], 0, keepdims=True)
        high = delta.astype(bf16).astype(f32)
        tail = jnp.where(extra == 0, high, jnp.where(extra == 1, delta - high, 0.0))
        dout_more = jnp.concatenate([dout, tail], 0).astype(bf16)
        values = jnp.concatenate([v, jnp.where(extra < 2, -1.0, 0.0)], 0).astype(bf16)
        dscores = weights.astype(f32) * mm(values, dout_more, TN)
        dround = dscores.astype(bf16)
        dvalue = mm(dout.astype(bf16), weights, NT)
        ones = jnp.where(extra == 0, 1.0, 0.0).astype(bf16)
        dquery = mm(jnp.concatenate([k_round, ones], 0), dround)
        excess = dquery[HEAD_DIM : HEAD_DIM + 1, :]
        dquery = dquery[:HEAD_DIM, :]
        dkey = mm(q_round, dround, NT)
        scale_out[pl.ds(head, 1), :] = (
            jnp.sum(q_round.astype(f32) * dquery, 0, keepdims=True) - means[head] * excess
        )
        dquery = dquery * factor
        dquery = (dquery - q_unit * jnp.sum(q_unit * dquery, 0, keepdims=True)) * q_inv
        dkey = (dkey - k_unit * jnp.sum(k_unit * dkey, 0, keepdims=True)) * k_inv
        send_ref[pl.ds(768 + at, HEAD_DIM), :] = dquery.astype(bf16)
        send_ref[pl.ds(768 + D + at, HEAD_DIM), :] = dkey.astype(bf16)
        send_ref[pl.ds(768 + 2 * D + at, HEAD_DIM), :] = dvalue.astype(bf16)
        total = None
        for b in range(8):
            near = dscores[(15 - b) * 16 : (15 - b) * 16 + 16, :]
            far = dscores[(7 - b) * 16 : (7 - b) * 16 + 16, :]
            wide = jnp.concatenate(
                [near[:, :128], near[:, 128:] + far[:, :128], far[:, 128:], jnp.zeros((16, 128), f32)], 1
            )
            if b:
                wide = pltpu.roll(wide, 16 * b, 1)
            total = wide if total is None else total + wide
        table_out[head] = total
        return carry

    lax.fori_loop(0, HEADS, backward_head, 0, unroll=24)

    dtokens = up[...] + mm(weight_ref[...], send_ref[768:3072, :]).T
    grid3[...] = dtokens.reshape(WIN, WIN, D)
    for (r, c), part in zip(places, (d00, d01, d10, d11)):
        part[...] = grid3[r : r + 8, c : c + 8, :].reshape(QUAD, D).astype(bf16)


def table_kernel(outer_ref, hidden_ref, slope_ref, table_ref, gain_ref, scale_ref, pack_ref, rows_ref, work_ref):
    first_coord, second_coord = slot_coords()
    hidden = hidden_ref[...]
    lane = lax.broadcasted_iota(jnp.int32, (HEADS, 512), 1)
    first = (lane % 32) < 16
    for head in range(HEADS):
        rows_ref[:, head : head + 1, :] = table_ref[head].reshape(WIN, 1, 512)
    even = jnp.zeros((HEADS, 512), f32)
    odd = jnp.zeros((HEADS, 512), f32)
    for cj in range(WIN):
        row = rows_ref[cj]
        even = even + pltpu.roll(jnp.where(first, row, 0.0), 15 - cj, 1)
        odd = odd + pltpu.roll(jnp.where(first, 0.0, row), (512 - 1 - cj) % 512, 1)
    dgrid = jnp.concatenate([even, odd], 1)
    dlogits = dgrid * slope_ref[...]
    outer = mm(dlogits, hidden, NN, exact)
    dhidden = mm(dlogits, outer_ref[...], TN, exact)
    dhidden = jnp.where(hidden > 0.0, dhidden, 0.0)
    scale = jnp.sum(scale_ref[...], -1, keepdims=True)
    where_row = lax.broadcasted_iota(jnp.int32, (HEADS, PART), 0)
    where_lane = lax.broadcasted_iota(jnp.int32, (HEADS, PART), 1)
    first_inner = jnp.sum(first_coord * dhidden, 0, keepdims=True)
    second_inner = jnp.sum(second_coord * dhidden, 0, keepdims=True)
    offset = jnp.sum(dhidden, 0, keepdims=True)
    work_ref[0:HEADS, :] = outer[:, :PART]
    for head in range(HEADS):
        place = (head % 3) * 128
        work_ref[24 + head // 3 : 25 + head // 3, place : place + 128] = outer[head : head + 1, PART:]
    work_ref[32:33, :] = first_inner[:, :PART]
    work_ref[33:34, :] = second_inner[:, :PART]
    work_ref[34:35, :] = jnp.concatenate([first_inner[:, PART:], second_inner[:, PART:], offset[:, PART:]], 1)
    work_ref[35:36, :] = offset[:, :PART]
    work_ref[36:37, :] = gain_ref[:, :PART]
    work_ref[37:38, :] = gain_ref[:, PART:]
    work_ref[38:39, :] = jnp.sum(jnp.where(where_row == where_lane, scale, 0.0), 0, keepdims=True)
    work_ref[39:64, :] = jnp.zeros((25, PART), f32)
    pack_ref[...] = work_ref[...].astype(bf16)


def grads_kernel(keep_ref, send_ref, got_ref, pack_ref, got_pack_ref, out_ref):
    pack = pack_ref[...].astype(f32) + got_pack_ref[...].astype(f32)
    for part in range(8):
        for hi in range(2):
            total = None
            for own, source in ((keep_ref, send_ref), (got_ref, got_ref)):
                base = hi * 192 + (384 if part >= 6 else 0)
                rows = own[base : base + 192, :]
                if part < 6:
                    piece = mm(rows, source[768 + part * PART : 768 + (part + 1) * PART, :], NT)
                else:
                    first = 3072 if part == 6 else 3072 + AREA
                    halves = [
                        mm(rows, source[first + n * AREA : first + (n + 1) * AREA, :]) for n in range(2)
                    ]
                    if part == 6:
                        piece = jnp.concatenate([halves[0], halves[1][:, :128]], 1)
                    else:
                        piece = jnp.concatenate([halves[0][:, 128:], halves[1]], 1)
                total = piece if total is None else total + piece
            out_ref[hi * 8 + part] = jnp.concatenate([total, pack[part * 8 : part * 8 + 8]], 0).astype(bf16)


def plane_kernel(in_ref, out_ref):
    total = in_ref[0].astype(f32)
    for n in range(1, 16):
        total = total + in_ref[n].astype(f32)
    for z in range(8):
        out_ref[z] = jnp.concatenate([total[z * BLOCK : (z + 1) * BLOCK], total[192:200]], 0).astype(bf16)


def column_kernel(in_ref, out_ref):
    total = in_ref[0].astype(f32)
    for n in range(1, 8):
        total = total + in_ref[n].astype(f32)
    both = total.astype(bf16)
    for n in range(8):
        out_ref[n] = both


def finish_kernel(in_ref, attend_ref, output_ref, gain_ref, scale_ref, inner_ref, offset_ref, outer_ref, work_ref):
    for part in range(8):
        piece = in_ref[part].astype(f32)
        if part < 6:
            attend_ref[:, part * PART : (part + 1) * PART] = piece[:BLOCK]
        else:
            output_ref[:, (part - 6) * PART : (part - 5) * PART] = piece[:BLOCK]
        work_ref[part * 8 : part * 8 + 8, :] = piece[24:32]
    tails = [
        work_ref[24 + head // 3 : 25 + head // 3, (head % 3) * 128 : (head % 3) * 128 + 128] for head in range(HEADS)
    ]
    outer = jnp.concatenate([work_ref[0:HEADS, :], jnp.concatenate(tails, 0)], 1)
    outer_ref[...] = outer
    inner_ref[0:1, :PART] = work_ref[32:33, :]
    inner_ref[1:2, :PART] = work_ref[33:34, :]
    inner_ref[0:1, PART:] = work_ref[34:35, 0:128]
    inner_ref[1:2, PART:] = work_ref[34:35, 128:256]
    offset_ref[...] = jnp.concatenate([work_ref[35:36, :], work_ref[34:35, 256:]], 1).reshape(HIDDEN)
    gain_ref[...] = jnp.concatenate([work_ref[36:37, :], work_ref[37:38, :]], 1).reshape(D)
    scale_ref[...] = work_ref[38:39, :].reshape(PART)[:HEADS]


def vmem(count):
    return [pl.BlockSpec(memory_space=pltpu.VMEM)] * count


HBM = pl.BlockSpec(memory_space=pltpu.MemorySpace.HBM)
SMEM = pl.BlockSpec(memory_space=pltpu.SMEM)


def params(mib):
    return pltpu.CompilerParams(vmem_limit_bytes=mib * 1024 * 1024)


def cost(micros):
    return pl.CostEstimate(flops=int(micros * 1.15e9), bytes_accessed=0, transcendentals=0)


def place_of(lat, hi, z, core):
    return lat * 32 + hi * 16 + z * 2 + core


def shift_pairs(lat_step, lon_step):
    return [
        (lat * 32 + lon, ((lat + lat_step) % 8) * 32 + (lon + lon_step) % 32)
        for lat in range(8)
        for lon in range(32)
    ]


PLANE = [[place_of(lat, hi, z, core) for hi in range(2) for lat in range(8)] for z in range(8) for core in range(2)]
COLUMN = [[place_of(lat, hi, z, core) for z in range(8)] for lat in range(8) for hi in range(2) for core in range(2)]
LATS = [[place_of(lat, hi, z, core) for lat in range(8)] for hi in range(2) for z in range(8) for core in range(2)]
CORES = [
    (place_of(lat, hi, z, core), place_of(lat, hi, z, 1 - core))
    for lat in range(8)
    for hi in range(2)
    for z in range(8)
    for core in range(2)
]


def exchange(value, groups):
    return lax.all_to_all(value, BOTH, 0, 0, axis_index_groups=groups, tiled=True)


def per_device(
    features, upstream, attend_weight, output_weight, norm_gain, logit_scale,
    table_inner, table_offset, table_outer, validity,
):
    steps = ((0, 0), (0, 1), (1, 0), (1, 1))
    both = pl.pallas_call(
        cut_kernel,
        out_shape=(jax.ShapeDtypeStruct((2 * QUAD, D), bf16),) * 4,
        in_specs=[HBM] * 2,
        out_specs=tuple(vmem(4)),
        scratch_shapes=[pltpu.VMEM((WIN, WIN, D), bf16)] * 2 + [pltpu.SemaphoreType.DMA((2,))],
        compiler_params=params(16),
        cost_estimate=cost(2),
        name="cut",
    )(features, upstream)
    moved = [
        value if step == (0, 0) else lax.ppermute(value, BOTH, shift_pairs(-step[0], -step[1]))
        for step, value in zip(steps, both)
    ]

    outer_t = table_outer.T
    offset_row = table_offset.reshape(1, HIDDEN)
    last = (lax.axis_index("lat") == lax.axis_size("lat") - 1).astype(jnp.int32).reshape(1)
    core = (lax.axis_index("lon") % 2).astype(jnp.int32).reshape(1)
    bias, mask, factor, hidden, slope, gain_row = pl.pallas_call(
        bias_kernel,
        out_shape=(
            jax.ShapeDtypeStruct((HEADS, WIN, 512), f32),
            jax.ShapeDtypeStruct((AREA, AREA), f32),
            jax.ShapeDtypeStruct((HEADS, 1, AREA), f32),
            jax.ShapeDtypeStruct((SLOTS, HIDDEN), f32),
            jax.ShapeDtypeStruct((HEADS, SLOTS), f32),
            jax.ShapeDtypeStruct((1, D), f32),
        ),
        in_specs=[SMEM] * 2 + vmem(5),
        out_specs=tuple(vmem(6)),
        scratch_shapes=[pltpu.VMEM((WIN, HEADS, 512), f32)],
        compiler_params=params(16),
        cost_estimate=cost(2),
        name="bias",
    )(last, logit_scale, table_inner, offset_row, outer_t, validity, norm_gain)

    quad_shape = jax.ShapeDtypeStruct((QUAD, D), bf16)
    send, keep, *dquads, gain_part, scale_part, table_part = pl.pallas_call(
        window_kernel,
        out_shape=(
            jax.ShapeDtypeStruct((3840, AREA), bf16),
            jax.ShapeDtypeStruct((768, AREA), bf16),
            quad_shape,
            quad_shape,
            quad_shape,
            quad_shape,
            jax.ShapeDtypeStruct((1, D), f32),
            jax.ShapeDtypeStruct((HEADS, AREA), f32),
            jax.ShapeDtypeStruct((HEADS, WIN, 512), f32),
        ),
        in_specs=[SMEM] + vmem(10),
        out_specs=tuple(vmem(9)),
        scratch_shapes=[
            pltpu.VMEM((WIN, WIN, D), f32),
            pltpu.VMEM((AREA, D), f32),
            pltpu.VMEM((D, AREA), f32),
            pltpu.VMEM((3 * D, AREA), f32),
            pltpu.VMEM((HEADS, AREA, AREA), bf16),
            pltpu.VMEM((HEADS, 1, AREA), f32),
            pltpu.VMEM((D, AREA), f32),
            pltpu.VMEM((D, AREA), bf16),
            pltpu.VMEM((HEADS, 1, AREA), f32),
        ],
        compiler_params=params(36),
        cost_estimate=cost(17),
        name="window",
    )(core, factor, bias, mask, *moved, gain_row, attend_weight, output_weight)

    got = lax.ppermute(send, BOTH, CORES)
    pack = pl.pallas_call(
        table_kernel,
        out_shape=jax.ShapeDtypeStruct((64, PART), bf16),
        in_specs=vmem(6),
        out_specs=vmem(1)[0],
        scratch_shapes=[pltpu.VMEM((WIN, HEADS, 512), f32), pltpu.VMEM((64, PART), f32)],
        compiler_params=params(16),
        cost_estimate=cost(5),
        name="table",
    )(outer_t, hidden, slope, table_part, gain_part, scale_part)
    got_pack = lax.ppermute(pack, BOTH, CORES)
    grads = pl.pallas_call(
        grads_kernel,
        out_shape=jax.ShapeDtypeStruct((16, 200, PART), bf16),
        in_specs=vmem(5),
        out_specs=vmem(1)[0],
        compiler_params=params(24),
        cost_estimate=cost(2),
        name="grads",
    )(keep, send, got, pack, got_pack)
    plane = pl.pallas_call(
        plane_kernel,
        out_shape=jax.ShapeDtypeStruct((8, 32, PART), bf16),
        in_specs=vmem(1),
        out_specs=vmem(1)[0],
        compiler_params=params(16),
        cost_estimate=cost(1),
        name="plane",
    )(exchange(grads, PLANE))
    late = lax.optimization_barrier((plane, *dquads))
    plane, dquads = late[0], late[1:]
    back = [
        value if step == (0, 0) else lax.ppermute(value, BOTH, shift_pairs(*step))
        for step, value in zip(steps, dquads)
    ]
    held = lax.optimization_barrier((exchange(plane, COLUMN), *back))
    column, back = held[0], held[1:]
    column = pl.pallas_call(
        column_kernel,
        out_shape=jax.ShapeDtypeStruct((8, 32, PART), bf16),
        in_specs=vmem(1),
        out_specs=vmem(1)[0],
        compiler_params=params(16),
        cost_estimate=cost(1),
        name="column",
    )(column)

    back = [value.reshape(SHIFT, SHIFT, D) for value in back]
    input_delta = jnp.concatenate(
        [jnp.concatenate([back[3], back[2]], 1), jnp.concatenate([back[1], back[0]], 1)], 0
    )
    column, input_delta = lax.optimization_barrier((column, input_delta))

    attend_delta, output_delta, gain, scale, inner, offset, outer = pl.pallas_call(
        finish_kernel,
        out_shape=(
            jax.ShapeDtypeStruct((BLOCK, 3 * D), f32),
            jax.ShapeDtypeStruct((BLOCK, D), f32),
            jax.ShapeDtypeStruct((D,), f32),
            jax.ShapeDtypeStruct((HEADS,), f32),
            jax.ShapeDtypeStruct((2, HIDDEN), f32),
            jax.ShapeDtypeStruct((HIDDEN,), f32),
            jax.ShapeDtypeStruct((HEADS, HIDDEN), f32),
        ),
        in_specs=vmem(1),
        out_specs=tuple(vmem(7)),
        scratch_shapes=[pltpu.VMEM((64, PART), f32)],
        compiler_params=params(16),
        cost_estimate=cost(1),
        name="finish",
    )(exchange(column, LATS))
    return (
        input_delta,
        attend_delta,
        output_delta,
        gain,
        scale,
        inner,
        offset,
        outer.T,
    )


def solution(mesh):
    in_specs = (
        P("lat", "lon", None),
        P("lat", "lon", None),
        P(),
        P(),
        P(),
        P(),
        P(),
        P(),
        P(),
        P("lat", "lon"),
    )
    out_specs = (P("lat", "lon", None), P("lon", None), P("lon", None), P(), P(), P(), P(), P())
    return jax.shard_map(
        per_device, mesh=mesh, in_specs=in_specs, out_specs=out_specs, check_vma=False
    )
```

```python
import functools

import jax
import jax.numpy as jnp
import numpy as np
from jax import lax
from jax.experimental import pallas as pl
from jax.experimental.pallas import tpu as pltpu
from jax.sharding import PartitionSpec as P

D = 768
HEADS = 24
HEAD_DIM = 32
HIDDEN = 512
WIN = 16
SHIFT = 8
AREA = WIN * WIN
QUAD = SHIFT * SHIFT
SLOTS = 1024
PART = 384
BLOCK = 24
BOTH = ("lat", "lon")
NEG = -1e30

f32 = jnp.float32
bf16 = jnp.bfloat16
exact = lax.Precision.HIGHEST

NN = (((1,), (0,)), ((), ()))
NT = (((1,), (1,)), ((), ()))
TN = (((0,), (0,)), ((), ()))


def mm(a, b, dims=NN, precision=None):
    return lax.dot_general(a, b, dims, precision=precision, preferred_element_type=f32)


def slot_coords():
    slot = lax.broadcasted_iota(jnp.int32, (SLOTS, 128), 0)
    row = (slot // 32) % 16 * 2 + slot // 512
    out = []
    for index in (row, slot % 32):
        spread = (index - (WIN - 1)).astype(f32) * (8.0 / (WIN - 1))
        size = jnp.log(1.0 + jnp.abs(spread)) * (1.0 / (3.0 * np.log(2.0)))
        out.append(jnp.concatenate([jnp.where(spread < 0.0, -size, size)] * 4, 1))
    return out


def hidden_of(inner_ref, offset_ref):
    first, second = slot_coords()
    return jnp.maximum(first * inner_ref[0:1, :] + second * inner_ref[1:2, :] + offset_ref[...], 0.0)


def fetch(pairs, sems, first=0):
    copies = [
        pltpu.make_async_copy(source, target, sems.at[first + n]) for n, (source, target) in enumerate(pairs)
    ]
    for copy in copies:
        copy.start()
    return copies


def cut_kernel(features_hbm, upstream_hbm, o00, o01, o10, o11, features_ref, upstream_ref, sems):
    outs = (o00, o01, o10, o11)
    for copy in fetch(((features_hbm, features_ref), (upstream_hbm, upstream_ref)), sems):
        copy.wait()
    feats = features_ref[...].astype(f32)
    ups = upstream_ref[...].astype(f32)
    for (r, c), out in zip(((8, 8), (8, 0), (0, 8), (0, 0)), outs):
        out[0:QUAD, :] = feats[r : r + 8, c : c + 8].reshape(QUAD, D).astype(bf16)
        out[QUAD:, :] = ups[r : r + 8, c : c + 8].reshape(QUAD, D).astype(bf16)


def bias_kernel(
    last_ref, log_ref, inner_ref, offset_ref, outer_ref, valid_ref, gain_ref,
    table_ref, mask_ref, factor_ref, hidden_ref, slope_ref, gain_out, rows_ref,
):
    gain_out[...] = gain_ref[...].reshape(1, D)
    hidden = hidden_of(inner_ref, offset_ref)
    hidden_ref[...] = hidden
    sig = jax.nn.sigmoid(mm(outer_ref[...], hidden, NT, exact))
    grid = 16.0 * sig
    slope_ref[...] = grid * (1.0 - sig)
    even = grid[:, :512]
    odd = grid[:, 512:]
    lane = lax.broadcasted_iota(jnp.int32, (HEADS, 512), 1)
    first = (lane % 32) < 16
    for cj in range(WIN):
        rows_ref[cj] = jnp.where(
            first,
            pltpu.roll(even, (512 - 15 + cj) % 512, 1),
            pltpu.roll(odd, (1 + cj) % 512, 1),
        )
    valid = valid_ref[...].astype(f32).T
    split = last_ref[0] == 1
    cj = lax.broadcasted_iota(jnp.int32, (WIN, AREA), 0)
    query = lax.broadcasted_iota(jnp.int32, (WIN, AREA), 1)
    for rj in range(WIN):
        same = jnp.logical_or((query >= AREA // 2) == (rj >= WIN // 2), jnp.logical_not(split))
        seen = jnp.logical_or(valid[:, rj : rj + 1] == 1.0, rj * WIN + cj == query)
        mask_ref[rj * WIN : (rj + 1) * WIN, :] = jnp.where(jnp.logical_and(same, seen), 0.0, NEG)

    for head in range(HEADS):
        factor_ref[head] = jnp.exp(jnp.full((1, AREA), log_ref[head], f32))
        table_ref[head] = rows_ref[:, head : head + 1, :].reshape(WIN, 512)


def window_kernel(
    core_ref, factor_ref, table_ref, mask_ref, q00, q01, q10, q11, gain_ref, weight_ref, out_weight_ref,
    send_ref, keep_ref, d00, d10, dlon, gain_out, scale_out, table_out,
    grid3, up, tokt, projt, exps, inv, hot, doutt, means,
):
    places = ((0, 0), (0, 8), (8, 0), (8, 8))
    quads = (q00, q01, q10, q11)

    def assemble(rows):
        for (r, c), part in zip(places, quads):
            grid3[r : r + 8, c : c + 8, :] = part[rows, :].astype(f32).reshape(8, 8, D)
        return grid3[...].reshape(AREA, D)

    def rows_of(source, core):
        pieces = []
        for hi in range(2):
            for z in range(8):
                at = pl.multiple_of((hi * 16 + z * 2 + core) * BLOCK, 8)
                pieces.append(source[pl.ds(at, BLOCK), :])
        return jnp.concatenate(pieces, 0).astype(bf16)

    mine = core_ref[0]
    up[...] = assemble(slice(QUAD, 2 * QUAD))
    tokens32 = assemble(slice(0, QUAD))
    tokens = tokens32.astype(bf16)
    tokt[...] = tokens32.T
    for part in range(6):
        cols = slice(part * PART, (part + 1) * PART)
        projt[cols, :] = mm(tokens, weight_ref[:, cols]).T
    keep_ref[0:384, :] = rows_of(tokt, mine)
    send_ref[0:384, :] = rows_of(tokt, 1 - mine)

    def head_inputs(head):
        at = pl.multiple_of(head * HEAD_DIM, HEAD_DIM)
        q = projt[pl.ds(at, HEAD_DIM), :]
        k = projt[pl.ds(D + at, HEAD_DIM), :]
        v = projt[pl.ds(2 * D + at, HEAD_DIM), :]
        q_inv = lax.rsqrt(jnp.sum(q * q, 0, keepdims=True) + 1.0)
        k_inv = lax.rsqrt(jnp.sum(k * k, 0, keepdims=True) + 1.0)
        q_unit = q * q_inv
        k_unit = k * k_inv
        factor = factor_ref[head]
        return at, q_unit, q_inv, (q_unit * factor).astype(bf16), k_unit, k_inv, k_unit.astype(bf16), v, factor

    extra = lax.broadcasted_iota(jnp.int32, (16, AREA), 0)

    def forward_head(head, carry):
        at, _, _, q_round, _, _, k_round, v, _ = head_inputs(head)
        scores = mm(k_round, q_round, TN)
        table = table_ref[head]
        slabs = [None] * WIN
        for b in range(8):
            turned = table if b == 0 else pltpu.roll(table, 512 - 16 * b, 1)
            for a in range(2):
                rj = 15 - (8 * a + b)
                rows = slice(rj * 16, rj * 16 + 16)
                slabs[rj] = jnp.exp(
                    scores[rows, :] + (turned[:, 128 * a : 128 * a + 256] + mask_ref[rows, :])
                ).astype(bf16)
        weights = jnp.concatenate(slabs, 0)
        exps[head] = weights
        values = jnp.concatenate([v, jnp.where(extra == 0, 1.0, 0.0)], 0).astype(bf16)
        mixed = mm(jnp.concatenate([values, k_round], 0), weights)
        inverse = 1.0 / mixed[HEAD_DIM : HEAD_DIM + 1, :]
        inv[head] = inverse
        means[head] = jnp.sum(q_round.astype(f32) * mixed[48:, :], 0, keepdims=True) * inverse
        hot[pl.ds(at, HEAD_DIM), :] = mixed[:HEAD_DIM, :] * inverse
        return carry

    lax.fori_loop(0, HEADS, forward_head, 0, unroll=24)

    keep_ref[384:768, :] = rows_of(hot, mine)
    send_ref[384:768, :] = rows_of(hot, 1 - mine)
    heads_out = hot[...].T.astype(bf16)
    mixed_out = mm(heads_out, out_weight_ref[...])
    centre = jnp.mean(mixed_out, -1, keepdims=True)
    shifted = mixed_out - centre
    inverse = lax.rsqrt(jnp.mean(shifted * shifted, -1, keepdims=True) + 1e-05)
    normed = shifted * inverse
    up_now = up[...]
    gain_out[...] = jnp.sum(up_now * normed, 0, keepdims=True)
    dnormed = up_now * gain_ref[...]
    dmixed = (
        dnormed
        - jnp.mean(dnormed, -1, keepdims=True)
        - normed * jnp.mean(dnormed * normed, -1, keepdims=True)
    ) * inverse
    dmixed = dmixed.astype(bf16)
    for part in range(3):
        send_ref[3072 + part * AREA : 3072 + (part + 1) * AREA, :] = dmixed[:, part * AREA : (part + 1) * AREA]
    doutt[...] = mm(out_weight_ref[...], dmixed, NT).astype(bf16)

    def backward_head(head, carry):
        at, q_unit, q_inv, q_round, k_unit, k_inv, k_round, v, factor = head_inputs(head)
        weights = exps[head]
        inverse = inv[head]
        dout = (doutt[pl.ds(at, HEAD_DIM), :].astype(f32) * inverse).astype(bf16).astype(f32)
        delta = jnp.sum(dout * hot[pl.ds(at, HEAD_DIM), :], 0, keepdims=True)
        high = delta.astype(bf16).astype(f32)
        tail = jnp.where(extra == 0, high, jnp.where(extra == 1, delta - high, 0.0))
        dout_more = jnp.concatenate([dout, tail], 0).astype(bf16)
        values = jnp.concatenate([v, jnp.where(extra < 2, -1.0, 0.0)], 0).astype(bf16)
        dscores = weights.astype(f32) * mm(values, dout_more, TN)
        dround = dscores.astype(bf16)
        dvalue = mm(dout.astype(bf16), weights, NT)
        ones = jnp.where(extra == 0, 1.0, 0.0).astype(bf16)
        dquery = mm(jnp.concatenate([k_round, ones], 0), dround)
        excess = dquery[HEAD_DIM : HEAD_DIM + 1, :]
        dquery = dquery[:HEAD_DIM, :]
        dkey = mm(q_round, dround, NT)
        scale_out[pl.ds(head, 1), :] = (
            jnp.sum(q_round.astype(f32) * dquery, 0, keepdims=True) - means[head] * excess
        )
        dquery = dquery * factor
        dquery = (dquery - q_unit * jnp.sum(q_unit * dquery, 0, keepdims=True)) * q_inv
        dkey = (dkey - k_unit * jnp.sum(k_unit * dkey, 0, keepdims=True)) * k_inv
        send_ref[pl.ds(768 + at, HEAD_DIM), :] = dquery.astype(bf16)
        send_ref[pl.ds(768 + D + at, HEAD_DIM), :] = dkey.astype(bf16)
        send_ref[pl.ds(768 + 2 * D + at, HEAD_DIM), :] = dvalue.astype(bf16)
        total = None
        for b in range(8):
            near = dscores[(15 - b) * 16 : (15 - b) * 16 + 16, :]
            far = dscores[(7 - b) * 16 : (7 - b) * 16 + 16, :]
            wide = jnp.concatenate(
                [near[:, :128], near[:, 128:] + far[:, :128], far[:, 128:], jnp.zeros((16, 128), f32)], 1
            )
            if b:
                wide = pltpu.roll(wide, 16 * b, 1)
            total = wide if total is None else total + wide
        table_out[head] = total
        return carry

    lax.fori_loop(0, HEADS, backward_head, 0, unroll=24)

    dtokens = up[...] + mm(weight_ref[...], send_ref[768:3072, :]).T
    grid3[...] = dtokens.reshape(WIN, WIN, D)
    pieces = [grid3[r : r + 8, c : c + 8, :].reshape(QUAD, D).astype(bf16) for r, c in places]
    d00[...] = pieces[0]
    d10[...] = pieces[2]
    dlon[0:QUAD, :] = pieces[1]
    dlon[QUAD:, :] = pieces[3]


def table_kernel(outer_ref, hidden_ref, slope_ref, table_ref, gain_ref, scale_ref, pack_ref, rows_ref, work_ref):
    first_coord, second_coord = slot_coords()
    hidden = hidden_ref[...]
    lane = lax.broadcasted_iota(jnp.int32, (HEADS, 512), 1)
    first = (lane % 32) < 16
    for head in range(HEADS):
        rows_ref[:, head : head + 1, :] = table_ref[head].reshape(WIN, 1, 512)
    even = jnp.zeros((HEADS, 512), f32)
    odd = jnp.zeros((HEADS, 512), f32)
    for cj in range(WIN):
        row = rows_ref[cj]
        even = even + pltpu.roll(jnp.where(first, row, 0.0), 15 - cj, 1)
        odd = odd + pltpu.roll(jnp.where(first, 0.0, row), (512 - 1 - cj) % 512, 1)
    dgrid = jnp.concatenate([even, odd], 1)
    dlogits = dgrid * slope_ref[...]
    outer = mm(dlogits, hidden, NN, exact)
    dhidden = mm(dlogits, outer_ref[...], TN, exact)
    dhidden = jnp.where(hidden > 0.0, dhidden, 0.0)
    scale = jnp.sum(scale_ref[...], -1, keepdims=True)
    where_row = lax.broadcasted_iota(jnp.int32, (HEADS, PART), 0)
    where_lane = lax.broadcasted_iota(jnp.int32, (HEADS, PART), 1)
    first_inner = jnp.sum(first_coord * dhidden, 0, keepdims=True)
    second_inner = jnp.sum(second_coord * dhidden, 0, keepdims=True)
    offset = jnp.sum(dhidden, 0, keepdims=True)
    work_ref[0:HEADS, :] = outer[:, :PART]
    for head in range(HEADS):
        place = (head % 3) * 128
        work_ref[24 + head // 3 : 25 + head // 3, place : place + 128] = outer[head : head + 1, PART:]
    work_ref[32:33, :] = first_inner[:, :PART]
    work_ref[33:34, :] = second_inner[:, :PART]
    work_ref[34:35, :] = jnp.concatenate([first_inner[:, PART:], second_inner[:, PART:], offset[:, PART:]], 1)
    work_ref[35:36, :] = offset[:, :PART]
    work_ref[36:37, :] = gain_ref[:, :PART]
    work_ref[37:38, :] = gain_ref[:, PART:]
    work_ref[38:39, :] = jnp.sum(jnp.where(where_row == where_lane, scale, 0.0), 0, keepdims=True)
    work_ref[39:64, :] = jnp.zeros((25, PART), f32)
    pack_ref[...] = work_ref[...].astype(bf16)


def grads_kernel(keep_ref, send_ref, got_ref, pack_ref, got_pack_ref, out_ref):
    pack = pack_ref[...].astype(f32) + got_pack_ref[...].astype(f32)
    for part in range(8):
        for hi in range(2):
            total = None
            for own, source in ((keep_ref, send_ref), (got_ref, got_ref)):
                base = hi * 192 + (384 if part >= 6 else 0)
                rows = own[base : base + 192, :]
                if part < 6:
                    piece = mm(rows, source[768 + part * PART : 768 + (part + 1) * PART, :], NT)
                else:
                    first = 3072 if part == 6 else 3072 + AREA
                    halves = [
                        mm(rows, source[first + n * AREA : first + (n + 1) * AREA, :]) for n in range(2)
                    ]
                    if part == 6:
                        piece = jnp.concatenate([halves[0], halves[1][:, :128]], 1)
                    else:
                        piece = jnp.concatenate([halves[0][:, 128:], halves[1]], 1)
                total = piece if total is None else total + piece
            out_ref[hi * 8 + part] = jnp.concatenate([total, pack[part * 8 : part * 8 + 8]], 0).astype(bf16)


def plane_kernel(in_ref, out_ref):
    total = in_ref[0].astype(f32)
    for n in range(1, 16):
        total = total + in_ref[n].astype(f32)
    for z in range(8):
        out_ref[z] = jnp.concatenate([total[z * BLOCK : (z + 1) * BLOCK], total[192:200]], 0).astype(bf16)


def column_kernel(in_ref, out_ref):
    total = in_ref[0].astype(f32)
    for n in range(1, 8):
        total = total + in_ref[n].astype(f32)
    both = total.astype(bf16)
    for n in range(8):
        out_ref[n] = both


def finish_kernel(in_ref, attend_ref, output_ref, gain_ref, scale_ref, inner_ref, offset_ref, outer_ref, work_ref):
    for part in range(8):
        piece = in_ref[part].astype(f32)
        if part < 6:
            attend_ref[:, part * PART : (part + 1) * PART] = piece[:BLOCK]
        else:
            output_ref[:, (part - 6) * PART : (part - 5) * PART] = piece[:BLOCK]
        work_ref[part * 8 : part * 8 + 8, :] = piece[24:32]
    tails = [
        work_ref[24 + head // 3 : 25 + head // 3, (head % 3) * 128 : (head % 3) * 128 + 128] for head in range(HEADS)
    ]
    outer = jnp.concatenate([work_ref[0:HEADS, :], jnp.concatenate(tails, 0)], 1)
    outer_ref[...] = outer
    inner_ref[0:1, :PART] = work_ref[32:33, :]
    inner_ref[1:2, :PART] = work_ref[33:34, :]
    inner_ref[0:1, PART:] = work_ref[34:35, 0:128]
    inner_ref[1:2, PART:] = work_ref[34:35, 128:256]
    offset_ref[...] = jnp.concatenate([work_ref[35:36, :], work_ref[34:35, 256:]], 1).reshape(HIDDEN)
    gain_ref[...] = jnp.concatenate([work_ref[36:37, :], work_ref[37:38, :]], 1).reshape(D)
    scale_ref[...] = work_ref[38:39, :].reshape(PART)[:HEADS]


def vmem(count):
    return [pl.BlockSpec(memory_space=pltpu.VMEM)] * count


HBM = pl.BlockSpec(memory_space=pltpu.MemorySpace.HBM)
SMEM = pl.BlockSpec(memory_space=pltpu.SMEM)


def params(mib):
    return pltpu.CompilerParams(vmem_limit_bytes=mib * 1024 * 1024)


def cost(micros):
    return pl.CostEstimate(flops=int(micros * 1.15e9), bytes_accessed=0, transcendentals=0)


def place_of(lat, hi, z, core):
    return lat * 32 + hi * 16 + z * 2 + core


def shift_pairs(lat_step, lon_step):
    return [
        (lat * 32 + lon, ((lat + lat_step) % 8) * 32 + (lon + lon_step) % 32)
        for lat in range(8)
        for lon in range(32)
    ]


PLANE = [[place_of(lat, hi, z, core) for hi in range(2) for lat in range(8)] for z in range(8) for core in range(2)]
COLUMN = [[place_of(lat, hi, z, core) for z in range(8)] for lat in range(8) for hi in range(2) for core in range(2)]
LATS = [[place_of(lat, hi, z, core) for lat in range(8)] for hi in range(2) for z in range(8) for core in range(2)]
CORES = [
    (place_of(lat, hi, z, core), place_of(lat, hi, z, 1 - core))
    for lat in range(8)
    for hi in range(2)
    for z in range(8)
    for core in range(2)
]


def exchange(value, groups):
    return lax.all_to_all(value, BOTH, 0, 0, axis_index_groups=groups, tiled=True)


def per_device(
    features, upstream, attend_weight, output_weight, norm_gain, logit_scale,
    table_inner, table_offset, table_outer, validity,
):
    steps = ((0, 0), (0, 1), (1, 0), (1, 1))
    both = pl.pallas_call(
        cut_kernel,
        out_shape=(jax.ShapeDtypeStruct((2 * QUAD, D), bf16),) * 4,
        in_specs=[HBM] * 2,
        out_specs=tuple(vmem(4)),
        scratch_shapes=[pltpu.VMEM((WIN, WIN, D), bf16)] * 2 + [pltpu.SemaphoreType.DMA((2,))],
        compiler_params=params(60),
        cost_estimate=cost(2),
        name="cut",
    )(features, upstream)
    moved = [
        value if step == (0, 0) else lax.ppermute(value, BOTH, shift_pairs(-step[0], -step[1]))
        for step, value in zip(steps, both)
    ]

    outer_t = table_outer.T
    offset_row = table_offset.reshape(1, HIDDEN)
    last = (lax.axis_index("lat") == lax.axis_size("lat") - 1).astype(jnp.int32).reshape(1)
    core = (lax.axis_index("lon") % 2).astype(jnp.int32).reshape(1)
    bias, mask, factor, hidden, slope, gain_row = pl.pallas_call(
        bias_kernel,
        out_shape=(
            jax.ShapeDtypeStruct((HEADS, WIN, 512), f32),
            jax.ShapeDtypeStruct((AREA, AREA), f32),
            jax.ShapeDtypeStruct((HEADS, 1, AREA), f32),
            jax.ShapeDtypeStruct((SLOTS, HIDDEN), f32),
            jax.ShapeDtypeStruct((HEADS, SLOTS), f32),
            jax.ShapeDtypeStruct((1, D), f32),
        ),
        in_specs=[SMEM] * 2 + vmem(5),
        out_specs=tuple(vmem(6)),
        scratch_shapes=[pltpu.VMEM((WIN, HEADS, 512), f32)],
        compiler_params=params(16),
        cost_estimate=cost(2),
        name="bias",
    )(last, logit_scale, table_inner, offset_row, outer_t, validity, norm_gain)

    quad_shape = jax.ShapeDtypeStruct((QUAD, D), bf16)
    send, keep, d00, d10, dlon, gain_part, scale_part, table_part = pl.pallas_call(
        window_kernel,
        out_shape=(
            jax.ShapeDtypeStruct((3840, AREA), bf16),
            jax.ShapeDtypeStruct((768, AREA), bf16),
            quad_shape,
            quad_shape,
            jax.ShapeDtypeStruct((2 * QUAD, D), bf16),
            jax.ShapeDtypeStruct((1, D), f32),
            jax.ShapeDtypeStruct((HEADS, AREA), f32),
            jax.ShapeDtypeStruct((HEADS, WIN, 512), f32),
        ),
        in_specs=[SMEM] + vmem(10),
        out_specs=tuple(vmem(8)),
        scratch_shapes=[
            pltpu.VMEM((WIN, WIN, D), f32),
            pltpu.VMEM((AREA, D), f32),
            pltpu.VMEM((D, AREA), f32),
            pltpu.VMEM((3 * D, AREA), f32),
            pltpu.VMEM((HEADS, AREA, AREA), bf16),
            pltpu.VMEM((HEADS, 1, AREA), f32),
            pltpu.VMEM((D, AREA), f32),
            pltpu.VMEM((D, AREA), bf16),
            pltpu.VMEM((HEADS, 1, AREA), f32),
        ],
        compiler_params=params(36),
        cost_estimate=cost(17),
        name="window",
    )(core, factor, bias, mask, *moved, gain_row, attend_weight, output_weight)

    got = lax.ppermute(send, BOTH, CORES)
    pack = pl.pallas_call(
        table_kernel,
        out_shape=jax.ShapeDtypeStruct((64, PART), bf16),
        in_specs=vmem(6),
        out_specs=vmem(1)[0],
        scratch_shapes=[pltpu.VMEM((WIN, HEADS, 512), f32), pltpu.VMEM((64, PART), f32)],
        compiler_params=params(16),
        cost_estimate=cost(5),
        name="table",
    )(outer_t, hidden, slope, table_part, gain_part, scale_part)
    got_pack = lax.ppermute(pack, BOTH, CORES)
    from_lon = lax.ppermute(dlon, BOTH, shift_pairs(0, 1))
    got_pack, from_lon = lax.optimization_barrier((got_pack, from_lon))
    grads = pl.pallas_call(
        grads_kernel,
        out_shape=jax.ShapeDtypeStruct((16, 200, PART), bf16),
        in_specs=vmem(5),
        out_specs=vmem(1)[0],
        compiler_params=params(24),
        cost_estimate=cost(2),
        name="grads",
    )(keep, send, got, pack, got_pack)
    plane = pl.pallas_call(
        plane_kernel,
        out_shape=jax.ShapeDtypeStruct((8, 32, PART), bf16),
        in_specs=vmem(1),
        out_specs=vmem(1)[0],
        compiler_params=params(16),
        cost_estimate=cost(1),
        name="plane",
    )(exchange(grads, PLANE))
    plane, d10, from_lon = lax.optimization_barrier((plane, d10, from_lon))
    from_lat = lax.ppermute(jnp.concatenate([d10, from_lon[QUAD:]], 0), BOTH, shift_pairs(1, 0))
    column, from_lat = lax.optimization_barrier((exchange(plane, COLUMN), from_lat))
    column = pl.pallas_call(
        column_kernel,
        out_shape=jax.ShapeDtypeStruct((8, 32, PART), bf16),
        in_specs=vmem(1),
        out_specs=vmem(1)[0],
        compiler_params=params(16),
        cost_estimate=cost(1),
        name="column",
    )(column)

    back = [value.reshape(SHIFT, SHIFT, D) for value in (d00, from_lon[:QUAD], from_lat[:QUAD], from_lat[QUAD:])]
    input_delta = jnp.concatenate(
        [jnp.concatenate([back[3], back[2]], 1), jnp.concatenate([back[1], back[0]], 1)], 0
    )
    column, input_delta = lax.optimization_barrier((column, input_delta))

    attend_delta, output_delta, gain, scale, inner, offset, outer = pl.pallas_call(
        finish_kernel,
        out_shape=(
            jax.ShapeDtypeStruct((BLOCK, 3 * D), f32),
            jax.ShapeDtypeStruct((BLOCK, D), f32),
            jax.ShapeDtypeStruct((D,), f32),
            jax.ShapeDtypeStruct((HEADS,), f32),
            jax.ShapeDtypeStruct((2, HIDDEN), f32),
            jax.ShapeDtypeStruct((HIDDEN,), f32),
            jax.ShapeDtypeStruct((HEADS, HIDDEN), f32),
        ),
        in_specs=vmem(1),
        out_specs=tuple(vmem(7)),
        scratch_shapes=[pltpu.VMEM((64, PART), f32)],
        compiler_params=params(16),
        cost_estimate=cost(1),
        name="finish",
    )(exchange(column, LATS))
    return (
        input_delta,
        attend_delta,
        output_delta,
        gain,
        scale,
        inner,
        offset,
        outer.T,
    )


def solution(mesh):
    in_specs = (
        P("lat", "lon", None),
        P("lat", "lon", None),
        P(),
        P(),
        P(),
        P(),
        P(),
        P(),
        P(),
        P("lat", "lon"),
    )
    out_specs = (P("lat", "lon", None), P("lon", None), P("lon", None), P(), P(), P(), P(), P())
    return jax.shard_map(
        per_device, mesh=mesh, in_specs=in_specs, out_specs=out_specs, check_vma=False
    )
```

```python
import functools

import jax
import jax.numpy as jnp
import numpy as np
from jax import lax
from jax.experimental import pallas as pl
from jax.experimental.pallas import tpu as pltpu
from jax.sharding import PartitionSpec as P

D = 768
HEADS = 24
HEAD_DIM = 32
HIDDEN = 512
WIN = 16
SHIFT = 8
AREA = WIN * WIN
QUAD = SHIFT * SHIFT
SLOTS = 1024
PART = 384
BLOCK = 24
BOTH = ("lat", "lon")
NEG = -1e30

f32 = jnp.float32
bf16 = jnp.bfloat16
exact = lax.Precision.HIGHEST

NN = (((1,), (0,)), ((), ()))
NT = (((1,), (1,)), ((), ()))
TN = (((0,), (0,)), ((), ()))


def mm(a, b, dims=NN, precision=None):
    return lax.dot_general(a, b, dims, precision=precision, preferred_element_type=f32)


def slot_coords():
    slot = lax.broadcasted_iota(jnp.int32, (SLOTS, 128), 0)
    row = (slot // 32) % 16 * 2 + slot // 512
    out = []
    for index in (row, slot % 32):
        spread = (index - (WIN - 1)).astype(f32) * (8.0 / (WIN - 1))
        size = jnp.log(1.0 + jnp.abs(spread)) * (1.0 / (3.0 * np.log(2.0)))
        out.append(jnp.concatenate([jnp.where(spread < 0.0, -size, size)] * 4, 1))
    return out


def hidden_of(inner_ref, offset_ref):
    first, second = slot_coords()
    return jnp.maximum(first * inner_ref[0:1, :] + second * inner_ref[1:2, :] + offset_ref[...], 0.0)


def fetch(pairs, sems, first=0):
    copies = [
        pltpu.make_async_copy(source, target, sems.at[first + n]) for n, (source, target) in enumerate(pairs)
    ]
    for copy in copies:
        copy.start()
    return copies


def cut_kernel(features_hbm, upstream_hbm, o00, o01, o10, o11, features_ref, upstream_ref, sems):
    outs = (o00, o01, o10, o11)
    for copy in fetch(((features_hbm, features_ref), (upstream_hbm, upstream_ref)), sems):
        copy.wait()
    feats = features_ref[...].astype(f32)
    ups = upstream_ref[...].astype(f32)
    for (r, c), out in zip(((8, 8), (8, 0), (0, 8), (0, 0)), outs):
        out[0:QUAD, :] = feats[r : r + 8, c : c + 8].reshape(QUAD, D).astype(bf16)
        out[QUAD:, :] = ups[r : r + 8, c : c + 8].reshape(QUAD, D).astype(bf16)


def bias_kernel(
    last_ref, log_ref, inner_ref, offset_ref, outer_ref, valid_ref, gain_ref,
    table_ref, mask_ref, factor_ref, high_ref, low_ref, slope_ref, gain_out, rows_ref,
):
    gain_out[...] = gain_ref[...].reshape(1, D)
    hidden = hidden_of(inner_ref, offset_ref)
    high = hidden.astype(bf16)
    high_ref[...] = high
    low_ref[...] = (hidden - high.astype(f32)).astype(bf16)
    sig = jax.nn.sigmoid(mm(outer_ref[...], hidden, NT, exact))
    grid = 16.0 * sig
    slope_ref[...] = grid * (1.0 - sig)
    even = grid[:, :512]
    odd = grid[:, 512:]
    lane = lax.broadcasted_iota(jnp.int32, (HEADS, 512), 1)
    first = (lane % 32) < 16
    for cj in range(WIN):
        rows_ref[cj] = jnp.where(
            first,
            pltpu.roll(even, (512 - 15 + cj) % 512, 1),
            pltpu.roll(odd, (1 + cj) % 512, 1),
        )
    valid = valid_ref[...].astype(f32).T
    split = last_ref[0] == 1
    cj = lax.broadcasted_iota(jnp.int32, (WIN, AREA), 0)
    query = lax.broadcasted_iota(jnp.int32, (WIN, AREA), 1)
    for rj in range(WIN):
        same = jnp.logical_or((query >= AREA // 2) == (rj >= WIN // 2), jnp.logical_not(split))
        seen = jnp.logical_or(valid[:, rj : rj + 1] == 1.0, rj * WIN + cj == query)
        mask_ref[rj * WIN : (rj + 1) * WIN, :] = jnp.where(jnp.logical_and(same, seen), 0.0, NEG)

    for head in range(HEADS):
        factor_ref[head] = jnp.exp(jnp.full((1, AREA), log_ref[head], f32))
        table_ref[head] = rows_ref[:, head : head + 1, :].reshape(WIN, 512)


def window_kernel(
    core_ref, factor_ref, table_ref, mask_ref, q00, q01, q10, q11, gain_ref, weight_ref, out_weight_ref,
    send_ref, keep_ref, d00, d10, dlon, gain_out, scale_out, table_out,
    grid3, up, tokt, projt, exps, inv, hot, doutt, means,
):
    places = ((0, 0), (0, 8), (8, 0), (8, 8))
    quads = (q00, q01, q10, q11)

    def assemble(rows):
        for (r, c), part in zip(places, quads):
            grid3[r : r + 8, c : c + 8, :] = part[rows, :].astype(f32).reshape(8, 8, D)
        return grid3[...].reshape(AREA, D)

    def rows_of(source, core):
        pieces = []
        for hi in range(2):
            for z in range(8):
                at = pl.multiple_of((hi * 16 + z * 2 + core) * BLOCK, 8)
                pieces.append(source[pl.ds(at, BLOCK), :])
        return jnp.concatenate(pieces, 0).astype(bf16)

    mine = core_ref[0]
    up[...] = assemble(slice(QUAD, 2 * QUAD))
    tokens32 = assemble(slice(0, QUAD))
    tokens = tokens32.astype(bf16)
    tokt[...] = tokens32.T
    for part in range(6):
        cols = slice(part * PART, (part + 1) * PART)
        projt[cols, :] = mm(tokens, weight_ref[:, cols]).T
    keep_ref[0:384, :] = rows_of(tokt, mine)
    send_ref[0:384, :] = rows_of(tokt, 1 - mine)

    def head_inputs(head):
        at = pl.multiple_of(head * HEAD_DIM, HEAD_DIM)
        q = projt[pl.ds(at, HEAD_DIM), :]
        k = projt[pl.ds(D + at, HEAD_DIM), :]
        v = projt[pl.ds(2 * D + at, HEAD_DIM), :]
        q_inv = lax.rsqrt(jnp.sum(q * q, 0, keepdims=True) + 1.0)
        k_inv = lax.rsqrt(jnp.sum(k * k, 0, keepdims=True) + 1.0)
        q_unit = q * q_inv
        k_unit = k * k_inv
        factor = factor_ref[head]
        return at, q_unit, q_inv, (q_unit * factor).astype(bf16), k_unit, k_inv, k_unit.astype(bf16), v, factor

    extra = lax.broadcasted_iota(jnp.int32, (16, AREA), 0)

    def forward_head(head, carry):
        at, _, _, q_round, _, _, k_round, v, _ = head_inputs(head)
        scores = mm(k_round, q_round, TN)
        table = table_ref[head]
        slabs = [None] * WIN
        for b in range(8):
            turned = table if b == 0 else pltpu.roll(table, 512 - 16 * b, 1)
            for a in range(2):
                rj = 15 - (8 * a + b)
                rows = slice(rj * 16, rj * 16 + 16)
                slabs[rj] = jnp.exp(
                    scores[rows, :] + (turned[:, 128 * a : 128 * a + 256] + mask_ref[rows, :])
                ).astype(bf16)
        weights = jnp.concatenate(slabs, 0)
        exps[head] = weights
        values = jnp.concatenate([v, jnp.where(extra == 0, 1.0, 0.0)], 0).astype(bf16)
        mixed = mm(jnp.concatenate([values, k_round], 0), weights)
        inverse = 1.0 / mixed[HEAD_DIM : HEAD_DIM + 1, :]
        inv[head] = inverse
        means[head] = jnp.sum(q_round.astype(f32) * mixed[48:, :], 0, keepdims=True) * inverse
        hot[pl.ds(at, HEAD_DIM), :] = mixed[:HEAD_DIM, :] * inverse
        return carry

    lax.fori_loop(0, HEADS, forward_head, 0, unroll=24)

    keep_ref[384:768, :] = rows_of(hot, mine)
    send_ref[384:768, :] = rows_of(hot, 1 - mine)
    heads_out = hot[...].T.astype(bf16)
    mixed_out = mm(heads_out, out_weight_ref[...])
    centre = jnp.mean(mixed_out, -1, keepdims=True)
    shifted = mixed_out - centre
    inverse = lax.rsqrt(jnp.mean(shifted * shifted, -1, keepdims=True) + 1e-05)
    normed = shifted * inverse
    up_now = up[...]
    gain_out[...] = jnp.sum(up_now * normed, 0, keepdims=True)
    dnormed = up_now * gain_ref[...]
    dmixed = (
        dnormed
        - jnp.mean(dnormed, -1, keepdims=True)
        - normed * jnp.mean(dnormed * normed, -1, keepdims=True)
    ) * inverse
    dmixed = dmixed.astype(bf16)
    for part in range(3):
        send_ref[3072 + part * AREA : 3072 + (part + 1) * AREA, :] = dmixed[:, part * AREA : (part + 1) * AREA]
    doutt[...] = mm(out_weight_ref[...], dmixed, NT).astype(bf16)

    def backward_head(head, carry):
        at, q_unit, q_inv, q_round, k_unit, k_inv, k_round, v, factor = head_inputs(head)
        weights = exps[head]
        inverse = inv[head]
        dout = (doutt[pl.ds(at, HEAD_DIM), :].astype(f32) * inverse).astype(bf16).astype(f32)
        delta = jnp.sum(dout * hot[pl.ds(at, HEAD_DIM), :], 0, keepdims=True)
        high = delta.astype(bf16).astype(f32)
        tail = jnp.where(extra == 0, high, jnp.where(extra == 1, delta - high, 0.0))
        dout_more = jnp.concatenate([dout, tail], 0).astype(bf16)
        values = jnp.concatenate([v, jnp.where(extra < 2, -1.0, 0.0)], 0).astype(bf16)
        dscores = weights.astype(f32) * mm(values, dout_more, TN)
        dround = dscores.astype(bf16)
        dvalue = mm(dout.astype(bf16), weights, NT)
        ones = jnp.where(extra == 0, 1.0, 0.0).astype(bf16)
        dquery = mm(jnp.concatenate([k_round, ones], 0), dround)
        excess = dquery[HEAD_DIM : HEAD_DIM + 1, :]
        dquery = dquery[:HEAD_DIM, :]
        dkey = mm(q_round, dround, NT)
        scale_out[pl.ds(head, 1), :] = (
            jnp.sum(q_round.astype(f32) * dquery, 0, keepdims=True) - means[head] * excess
        )
        dquery = dquery * factor
        dquery = (dquery - q_unit * jnp.sum(q_unit * dquery, 0, keepdims=True)) * q_inv
        dkey = (dkey - k_unit * jnp.sum(k_unit * dkey, 0, keepdims=True)) * k_inv
        send_ref[pl.ds(768 + at, HEAD_DIM), :] = dquery.astype(bf16)
        send_ref[pl.ds(768 + D + at, HEAD_DIM), :] = dkey.astype(bf16)
        send_ref[pl.ds(768 + 2 * D + at, HEAD_DIM), :] = dvalue.astype(bf16)
        total = None
        for b in range(8):
            near = dscores[(15 - b) * 16 : (15 - b) * 16 + 16, :]
            far = dscores[(7 - b) * 16 : (7 - b) * 16 + 16, :]
            wide = jnp.concatenate(
                [near[:, :128], near[:, 128:] + far[:, :128], far[:, 128:], jnp.zeros((16, 128), f32)], 1
            )
            if b:
                wide = pltpu.roll(wide, 16 * b, 1)
            total = wide if total is None else total + wide
        table_out[head] = total
        return carry

    lax.fori_loop(0, HEADS, backward_head, 0, unroll=24)

    dtokens = up[...] + mm(weight_ref[...], send_ref[768:3072, :]).T
    grid3[...] = dtokens.reshape(WIN, WIN, D)
    pieces = [grid3[r : r + 8, c : c + 8, :].reshape(QUAD, D).astype(bf16) for r, c in places]
    d00[...] = pieces[0]
    d10[...] = pieces[2]
    dlon[0:QUAD, :] = pieces[1]
    dlon[QUAD:, :] = pieces[3]


def table_kernel(
    outer_ref, high_ref, low_ref, slope_ref, table_ref, gain_ref, scale_ref, pack_ref, rows_ref, work_ref
):
    first_coord, second_coord = slot_coords()
    lane = lax.broadcasted_iota(jnp.int32, (HEADS, 512), 1)
    first = (lane % 32) < 16
    for head in range(HEADS):
        rows_ref[:, head : head + 1, :] = table_ref[head].reshape(WIN, 1, 512)
    even = jnp.zeros((HEADS, 512), f32)
    odd = jnp.zeros((HEADS, 512), f32)
    for cj in range(WIN):
        row = rows_ref[cj]
        even = even + pltpu.roll(jnp.where(first, row, 0.0), 15 - cj, 1)
        odd = odd + pltpu.roll(jnp.where(first, 0.0, row), (512 - 1 - cj) % 512, 1)
    dgrid = jnp.concatenate([even, odd], 1)
    dlogits = dgrid * slope_ref[...]
    top = dlogits.astype(bf16).astype(f32)
    rest = dlogits - top
    pair = jnp.concatenate([top, rest], 0).astype(bf16)
    high = high_ref[...]
    outer = mm(pair, high)
    outer = outer[:HEADS] + outer[HEADS:] + mm(pair, low_ref[...])[:HEADS]
    weight = outer_ref[...]
    weight_top = weight.astype(bf16).astype(f32)
    zeros = jnp.zeros((8, SLOTS), f32)
    left = jnp.concatenate([top, rest, top, zeros], 0).astype(bf16)
    right = jnp.concatenate([weight_top, weight_top, weight - weight_top, zeros[:, :HIDDEN]], 0).astype(bf16)
    dhidden = jnp.where(high.astype(f32) > 0.0, mm(left, right, TN), 0.0)
    scale = jnp.sum(scale_ref[...], -1, keepdims=True)
    where_row = lax.broadcasted_iota(jnp.int32, (HEADS, PART), 0)
    where_lane = lax.broadcasted_iota(jnp.int32, (HEADS, PART), 1)
    first_inner = jnp.sum(first_coord * dhidden, 0, keepdims=True)
    second_inner = jnp.sum(second_coord * dhidden, 0, keepdims=True)
    offset = jnp.sum(dhidden, 0, keepdims=True)
    work_ref[0:HEADS, :] = outer[:, :PART]
    for head in range(HEADS):
        place = (head % 3) * 128
        work_ref[24 + head // 3 : 25 + head // 3, place : place + 128] = outer[head : head + 1, PART:]
    work_ref[32:33, :] = first_inner[:, :PART]
    work_ref[33:34, :] = second_inner[:, :PART]
    work_ref[34:35, :] = jnp.concatenate([first_inner[:, PART:], second_inner[:, PART:], offset[:, PART:]], 1)
    work_ref[35:36, :] = offset[:, :PART]
    work_ref[36:37, :] = gain_ref[:, :PART]
    work_ref[37:38, :] = gain_ref[:, PART:]
    work_ref[38:39, :] = jnp.sum(jnp.where(where_row == where_lane, scale, 0.0), 0, keepdims=True)
    work_ref[39:64, :] = jnp.zeros((25, PART), f32)
    pack_ref[...] = work_ref[...].astype(bf16)


def grads_kernel(keep_ref, send_ref, got_ref, pack_ref, got_pack_ref, out_ref):
    pack = pack_ref[...].astype(f32) + got_pack_ref[...].astype(f32)
    for part in range(8):
        for hi in range(2):
            total = None
            for own, source in ((keep_ref, send_ref), (got_ref, got_ref)):
                base = hi * 192 + (384 if part >= 6 else 0)
                rows = own[base : base + 192, :]
                if part < 6:
                    piece = mm(rows, source[768 + part * PART : 768 + (part + 1) * PART, :], NT)
                else:
                    first = 3072 if part == 6 else 3072 + AREA
                    halves = [
                        mm(rows, source[first + n * AREA : first + (n + 1) * AREA, :]) for n in range(2)
                    ]
                    if part == 6:
                        piece = jnp.concatenate([halves[0], halves[1][:, :128]], 1)
                    else:
                        piece = jnp.concatenate([halves[0][:, 128:], halves[1]], 1)
                total = piece if total is None else total + piece
            out_ref[hi * 8 + part] = jnp.concatenate([total, pack[part * 8 : part * 8 + 8]], 0).astype(bf16)


def plane_kernel(in_ref, out_ref):
    total = in_ref[0].astype(f32)
    for n in range(1, 16):
        total = total + in_ref[n].astype(f32)
    for z in range(8):
        out_ref[z] = jnp.concatenate([total[z * BLOCK : (z + 1) * BLOCK], total[192:200]], 0).astype(bf16)


def column_kernel(in_ref, out_ref):
    total = in_ref[0].astype(f32)
    for n in range(1, 8):
        total = total + in_ref[n].astype(f32)
    both = total.astype(bf16)
    for n in range(8):
        out_ref[n] = both


def finish_kernel(in_ref, attend_ref, output_ref, gain_ref, scale_ref, inner_ref, offset_ref, outer_ref, work_ref):
    for part in range(8):
        piece = in_ref[part].astype(f32)
        if part < 6:
            attend_ref[:, part * PART : (part + 1) * PART] = piece[:BLOCK]
        else:
            output_ref[:, (part - 6) * PART : (part - 5) * PART] = piece[:BLOCK]
        work_ref[part * 8 : part * 8 + 8, :] = piece[24:32]
    tails = [
        work_ref[24 + head // 3 : 25 + head // 3, (head % 3) * 128 : (head % 3) * 128 + 128] for head in range(HEADS)
    ]
    outer = jnp.concatenate([work_ref[0:HEADS, :], jnp.concatenate(tails, 0)], 1)
    outer_ref[...] = outer
    inner_ref[0:1, :PART] = work_ref[32:33, :]
    inner_ref[1:2, :PART] = work_ref[33:34, :]
    inner_ref[0:1, PART:] = work_ref[34:35, 0:128]
    inner_ref[1:2, PART:] = work_ref[34:35, 128:256]
    offset_ref[...] = jnp.concatenate([work_ref[35:36, :], work_ref[34:35, 256:]], 1).reshape(HIDDEN)
    gain_ref[...] = jnp.concatenate([work_ref[36:37, :], work_ref[37:38, :]], 1).reshape(D)
    scale_ref[...] = work_ref[38:39, :].reshape(PART)[:HEADS]


def vmem(count):
    return [pl.BlockSpec(memory_space=pltpu.VMEM)] * count


HBM = pl.BlockSpec(memory_space=pltpu.MemorySpace.HBM)
SMEM = pl.BlockSpec(memory_space=pltpu.SMEM)


def params(mib):
    return pltpu.CompilerParams(vmem_limit_bytes=mib * 1024 * 1024)


def cost(micros):
    return pl.CostEstimate(flops=int(micros * 1.15e9), bytes_accessed=0, transcendentals=0)


def place_of(lat, hi, z, core):
    return lat * 32 + hi * 16 + z * 2 + core


def shift_pairs(lat_step, lon_step):
    return [
        (lat * 32 + lon, ((lat + lat_step) % 8) * 32 + (lon + lon_step) % 32)
        for lat in range(8)
        for lon in range(32)
    ]


PLANE = [[place_of(lat, hi, z, core) for hi in range(2) for lat in range(8)] for z in range(8) for core in range(2)]
COLUMN = [[place_of(lat, hi, z, core) for z in range(8)] for lat in range(8) for hi in range(2) for core in range(2)]
LATS = [[place_of(lat, hi, z, core) for lat in range(8)] for hi in range(2) for z in range(8) for core in range(2)]
CORES = [
    (place_of(lat, hi, z, core), place_of(lat, hi, z, 1 - core))
    for lat in range(8)
    for hi in range(2)
    for z in range(8)
    for core in range(2)
]


def exchange(value, groups):
    return lax.all_to_all(value, BOTH, 0, 0, axis_index_groups=groups, tiled=True)


def per_device(
    features, upstream, attend_weight, output_weight, norm_gain, logit_scale,
    table_inner, table_offset, table_outer, validity,
):
    steps = ((0, 0), (0, 1), (1, 0), (1, 1))
    both = pl.pallas_call(
        cut_kernel,
        out_shape=(jax.ShapeDtypeStruct((2 * QUAD, D), bf16),) * 4,
        in_specs=[HBM] * 2,
        out_specs=tuple(vmem(4)),
        scratch_shapes=[pltpu.VMEM((WIN, WIN, D), bf16)] * 2 + [pltpu.SemaphoreType.DMA((2,))],
        compiler_params=params(60),
        cost_estimate=cost(2),
        name="cut",
    )(features, upstream)
    moved = [both[0], None, None, None]
    for n in (3, 2, 1):
        moved[n] = lax.ppermute(both[n], BOTH, shift_pairs(-steps[n][0], -steps[n][1]))

    outer_t = table_outer.T
    offset_row = table_offset.reshape(1, HIDDEN)
    last = (lax.axis_index("lat") == lax.axis_size("lat") - 1).astype(jnp.int32).reshape(1)
    core = (lax.axis_index("lon") % 2).astype(jnp.int32).reshape(1)
    bias, mask, factor, hidden_high, hidden_low, slope, gain_row = pl.pallas_call(
        bias_kernel,
        out_shape=(
            jax.ShapeDtypeStruct((HEADS, WIN, 512), f32),
            jax.ShapeDtypeStruct((AREA, AREA), f32),
            jax.ShapeDtypeStruct((HEADS, 1, AREA), f32),
            jax.ShapeDtypeStruct((SLOTS, HIDDEN), bf16),
            jax.ShapeDtypeStruct((SLOTS, HIDDEN), bf16),
            jax.ShapeDtypeStruct((HEADS, SLOTS), f32),
            jax.ShapeDtypeStruct((1, D), f32),
        ),
        in_specs=[SMEM] * 2 + vmem(5),
        out_specs=tuple(vmem(7)),
        scratch_shapes=[pltpu.VMEM((WIN, HEADS, 512), f32)],
        compiler_params=params(16),
        cost_estimate=cost(2),
        name="bias",
    )(last, logit_scale, table_inner, offset_row, outer_t, validity, norm_gain)

    quad_shape = jax.ShapeDtypeStruct((QUAD, D), bf16)
    send, keep, d00, d10, dlon, gain_part, scale_part, table_part = pl.pallas_call(
        window_kernel,
        out_shape=(
            jax.ShapeDtypeStruct((3840, AREA), bf16),
            jax.ShapeDtypeStruct((768, AREA), bf16),
            quad_shape,
            quad_shape,
            jax.ShapeDtypeStruct((2 * QUAD, D), bf16),
            jax.ShapeDtypeStruct((1, D), f32),
            jax.ShapeDtypeStruct((HEADS, AREA), f32),
            jax.ShapeDtypeStruct((HEADS, WIN, 512), f32),
        ),
        in_specs=[SMEM] + vmem(10),
        out_specs=tuple(vmem(8)),
        scratch_shapes=[
            pltpu.VMEM((WIN, WIN, D), f32),
            pltpu.VMEM((AREA, D), f32),
            pltpu.VMEM((D, AREA), f32),
            pltpu.VMEM((3 * D, AREA), f32),
            pltpu.VMEM((HEADS, AREA, AREA), bf16),
            pltpu.VMEM((HEADS, 1, AREA), f32),
            pltpu.VMEM((D, AREA), f32),
            pltpu.VMEM((D, AREA), bf16),
            pltpu.VMEM((HEADS, 1, AREA), f32),
        ],
        compiler_params=params(36),
        cost_estimate=cost(17),
        name="window",
    )(core, factor, bias, mask, *moved, gain_row, attend_weight, output_weight)

    got = lax.ppermute(send, BOTH, CORES)
    pack = pl.pallas_call(
        table_kernel,
        out_shape=jax.ShapeDtypeStruct((64, PART), bf16),
        in_specs=vmem(7),
        out_specs=vmem(1)[0],
        scratch_shapes=[pltpu.VMEM((WIN, HEADS, 512), f32), pltpu.VMEM((64, PART), f32)],
        compiler_params=params(16),
        cost_estimate=cost(5),
        name="table",
    )(outer_t, hidden_high, hidden_low, slope, table_part, gain_part, scale_part)
    got_pack = lax.ppermute(pack, BOTH, CORES)
    from_lon = lax.ppermute(dlon, BOTH, shift_pairs(0, 1))
    got_pack, from_lon = lax.optimization_barrier((got_pack, from_lon))
    grads = pl.pallas_call(
        grads_kernel,
        out_shape=jax.ShapeDtypeStruct((16, 200, PART), bf16),
        in_specs=vmem(5),
        out_specs=vmem(1)[0],
        compiler_params=params(24),
        cost_estimate=cost(2),
        name="grads",
    )(keep, send, got, pack, got_pack)
    plane = pl.pallas_call(
        plane_kernel,
        out_shape=jax.ShapeDtypeStruct((8, 32, PART), bf16),
        in_specs=vmem(1),
        out_specs=vmem(1)[0],
        compiler_params=params(16),
        cost_estimate=cost(1),
        name="plane",
    )(exchange(grads, PLANE))
    plane, d10, from_lon = lax.optimization_barrier((plane, d10, from_lon))
    from_lat = lax.ppermute(jnp.concatenate([d10, from_lon[QUAD:]], 0), BOTH, shift_pairs(1, 0))
    column, from_lat = lax.optimization_barrier((exchange(plane, COLUMN), from_lat))
    column = pl.pallas_call(
        column_kernel,
        out_shape=jax.ShapeDtypeStruct((8, 32, PART), bf16),
        in_specs=vmem(1),
        out_specs=vmem(1)[0],
        compiler_params=params(16),
        cost_estimate=cost(1),
        name="column",
    )(column)

    back = [value.reshape(SHIFT, SHIFT, D) for value in (d00, from_lon[:QUAD], from_lat[:QUAD], from_lat[QUAD:])]
    input_delta = jnp.concatenate(
        [jnp.concatenate([back[3], back[2]], 1), jnp.concatenate([back[1], back[0]], 1)], 0
    )
    column, input_delta = lax.optimization_barrier((column, input_delta))

    attend_delta, output_delta, gain, scale, inner, offset, outer = pl.pallas_call(
        finish_kernel,
        out_shape=(
            jax.ShapeDtypeStruct((BLOCK, 3 * D), f32),
            jax.ShapeDtypeStruct((BLOCK, D), f32),
            jax.ShapeDtypeStruct((D,), f32),
            jax.ShapeDtypeStruct((HEADS,), f32),
            jax.ShapeDtypeStruct((2, HIDDEN), f32),
            jax.ShapeDtypeStruct((HIDDEN,), f32),
            jax.ShapeDtypeStruct((HEADS, HIDDEN), f32),
        ),
        in_specs=vmem(1),
        out_specs=tuple(vmem(7)),
        scratch_shapes=[pltpu.VMEM((64, PART), f32)],
        compiler_params=params(16),
        cost_estimate=cost(1),
        name="finish",
    )(exchange(column, LATS))
    return (
        input_delta,
        attend_delta,
        output_delta,
        gain,
        scale,
        inner,
        offset,
        outer.T,
    )


def solution(mesh):
    in_specs = (
        P("lat", "lon", None),
        P("lat", "lon", None),
        P(),
        P(),
        P(),
        P(),
        P(),
        P(),
        P(),
        P("lat", "lon"),
    )
    out_specs = (P("lat", "lon", None), P("lon", None), P("lon", None), P(), P(), P(), P(), P())
    return jax.shard_map(
        per_device, mesh=mesh, in_specs=in_specs, out_specs=out_specs, check_vma=False
    )
```

```python
import functools

import jax
import jax.numpy as jnp
import numpy as np
from jax import lax
from jax.experimental import pallas as pl
from jax.experimental.pallas import tpu as pltpu
from jax.sharding import PartitionSpec as P

D = 768
HEADS = 24
HEAD_DIM = 32
HIDDEN = 512
WIN = 16
SHIFT = 8
AREA = WIN * WIN
QUAD = SHIFT * SHIFT
SLOTS = 1024
PART = 384
BLOCK = 24
BOTH = ("lat", "lon")
NEG = -1e30

f32 = jnp.float32
bf16 = jnp.bfloat16
exact = lax.Precision.HIGHEST

NN = (((1,), (0,)), ((), ()))
NT = (((1,), (1,)), ((), ()))
TN = (((0,), (0,)), ((), ()))


def mm(a, b, dims=NN, precision=None):
    return lax.dot_general(a, b, dims, precision=precision, preferred_element_type=f32)


def slot_coords():
    slot = lax.broadcasted_iota(jnp.int32, (SLOTS, 128), 0)
    row = (slot // 32) % 16 * 2 + slot // 512
    out = []
    for index in (row, slot % 32):
        spread = (index - (WIN - 1)).astype(f32) * (8.0 / (WIN - 1))
        size = jnp.log(1.0 + jnp.abs(spread)) * (1.0 / (3.0 * np.log(2.0)))
        out.append(jnp.concatenate([jnp.where(spread < 0.0, -size, size)] * 4, 1))
    return out


def hidden_of(inner_ref, offset_ref):
    first, second = slot_coords()
    return jnp.maximum(first * inner_ref[0:1, :] + second * inner_ref[1:2, :] + offset_ref[...], 0.0)


def fetch(pairs, sems, first=0):
    copies = [
        pltpu.make_async_copy(source, target, sems.at[first + n]) for n, (source, target) in enumerate(pairs)
    ]
    for copy in copies:
        copy.start()
    return copies


def cut_kernel(features_hbm, upstream_hbm, o00, o01, o10, o11, features_ref, upstream_ref, sems):
    outs = (o00, o01, o10, o11)
    for copy in fetch(((features_hbm, features_ref), (upstream_hbm, upstream_ref)), sems):
        copy.wait()
    feats = features_ref[...].astype(f32)
    ups = upstream_ref[...].astype(f32)
    for (r, c), out in zip(((8, 8), (8, 0), (0, 8), (0, 0)), outs):
        out[0:QUAD, :] = feats[r : r + 8, c : c + 8].reshape(QUAD, D).astype(bf16)
        out[QUAD:, :] = ups[r : r + 8, c : c + 8].reshape(QUAD, D).astype(bf16)


def bias_kernel(
    last_ref, log_ref, inner_ref, offset_ref, outer_ref, valid_ref, gain_ref,
    table_ref, mask_ref, factor_ref, high_ref, low_ref, slope_ref, gain_out, rows_ref,
):
    gain_out[...] = gain_ref[...].reshape(1, D)
    hidden = hidden_of(inner_ref, offset_ref)
    high = hidden.astype(bf16)
    high_ref[...] = high
    low_ref[...] = (hidden - high.astype(f32)).astype(bf16)
    sig = jax.nn.sigmoid(mm(outer_ref[...], hidden, NT, exact))
    grid = 16.0 * sig
    slope_ref[...] = grid * (1.0 - sig)
    even = grid[:, :512]
    odd = grid[:, 512:]
    lane = lax.broadcasted_iota(jnp.int32, (HEADS, 512), 1)
    first = (lane % 32) < 16
    for cj in range(WIN):
        rows_ref[cj] = jnp.where(
            first,
            pltpu.roll(even, (512 - 15 + cj) % 512, 1),
            pltpu.roll(odd, (1 + cj) % 512, 1),
        )
    valid = valid_ref[...].astype(f32).T
    split = last_ref[0] == 1
    cj = lax.broadcasted_iota(jnp.int32, (WIN, AREA), 0)
    query = lax.broadcasted_iota(jnp.int32, (WIN, AREA), 1)
    for rj in range(WIN):
        same = jnp.logical_or((query >= AREA // 2) == (rj >= WIN // 2), jnp.logical_not(split))
        seen = jnp.logical_or(valid[:, rj : rj + 1] == 1.0, rj * WIN + cj == query)
        mask_ref[rj * WIN : (rj + 1) * WIN, :] = jnp.where(jnp.logical_and(same, seen), 0.0, NEG)

    for head in range(HEADS):
        factor_ref[head] = jnp.exp(jnp.full((1, AREA), log_ref[head], f32))
        table_ref[head] = rows_ref[:, head : head + 1, :].reshape(WIN, 512)


def window_kernel(
    core_ref, factor_ref, table_ref, mask_ref, q00, q01, q10, q11, gain_ref, weight_ref, out_weight_ref,
    send_ref, keep_ref, d00, d10, dlon, gain_out, scale_out, table_out,
    grid3, up, tokt, projt, exps, inv, hot, doutt, means,
):
    places = ((0, 0), (0, 8), (8, 0), (8, 8))
    quads = (q00, q01, q10, q11)

    def assemble(rows):
        for (r, c), part in zip(places, quads):
            grid3[r : r + 8, c : c + 8, :] = part[rows, :].astype(f32).reshape(8, 8, D)
        return grid3[...].reshape(AREA, D)

    def rows_of(source, core):
        pieces = []
        for hi in range(2):
            for z in range(8):
                at = pl.multiple_of((hi * 16 + z * 2 + core) * BLOCK, 8)
                pieces.append(source[pl.ds(at, BLOCK), :])
        return jnp.concatenate(pieces, 0).astype(bf16)

    mine = core_ref[0]
    up[...] = assemble(slice(QUAD, 2 * QUAD))
    tokens32 = assemble(slice(0, QUAD))
    tokens = tokens32.astype(bf16)
    tokt[...] = tokens32.T
    for part in range(6):
        cols = slice(part * PART, (part + 1) * PART)
        projt[cols, :] = mm(tokens, weight_ref[:, cols]).T
    keep_ref[0:384, :] = rows_of(tokt, mine)
    send_ref[0:384, :] = rows_of(tokt, 1 - mine)

    def head_inputs(head):
        at = pl.multiple_of(head * HEAD_DIM, HEAD_DIM)
        q = projt[pl.ds(at, HEAD_DIM), :]
        k = projt[pl.ds(D + at, HEAD_DIM), :]
        v = projt[pl.ds(2 * D + at, HEAD_DIM), :]
        q_inv = lax.rsqrt(jnp.sum(q * q, 0, keepdims=True) + 1.0)
        k_inv = lax.rsqrt(jnp.sum(k * k, 0, keepdims=True) + 1.0)
        q_unit = q * q_inv
        k_unit = k * k_inv
        factor = factor_ref[head]
        return at, q_unit, q_inv, (q_unit * factor).astype(bf16), k_unit, k_inv, k_unit.astype(bf16), v, factor

    extra = lax.broadcasted_iota(jnp.int32, (16, AREA), 0)

    def forward_head(head, carry):
        at, _, _, q_round, _, _, k_round, v, _ = head_inputs(head)
        scores = mm(k_round, q_round, TN)
        table = table_ref[head]
        slabs = [None] * WIN
        for b in range(8):
            turned = table if b == 0 else pltpu.roll(table, 512 - 16 * b, 1)
            for a in range(2):
                rj = 15 - (8 * a + b)
                rows = slice(rj * 16, rj * 16 + 16)
                slabs[rj] = jnp.exp(
                    scores[rows, :] + (turned[:, 128 * a : 128 * a + 256] + mask_ref[rows, :])
                ).astype(bf16)
        weights = jnp.concatenate(slabs, 0)
        exps[head] = weights
        values = jnp.concatenate([v, jnp.where(extra == 0, 1.0, 0.0)], 0).astype(bf16)
        mixed = mm(jnp.concatenate([values, k_round], 0), weights)
        inverse = 1.0 / mixed[HEAD_DIM : HEAD_DIM + 1, :]
        inv[head] = inverse
        means[head] = jnp.sum(q_round.astype(f32) * mixed[48:, :], 0, keepdims=True) * inverse
        hot[pl.ds(at, HEAD_DIM), :] = mixed[:HEAD_DIM, :] * inverse
        return carry

    lax.fori_loop(0, HEADS, forward_head, 0, unroll=24)

    keep_ref[384:768, :] = rows_of(hot, mine)
    send_ref[384:768, :] = rows_of(hot, 1 - mine)
    heads_out = hot[...].T.astype(bf16)
    mixed_out = mm(heads_out, out_weight_ref[...])
    centre = jnp.mean(mixed_out, -1, keepdims=True)
    shifted = mixed_out - centre
    inverse = lax.rsqrt(jnp.mean(shifted * shifted, -1, keepdims=True) + 1e-05)
    normed = shifted * inverse
    up_now = up[...]
    gain_out[...] = jnp.sum(up_now * normed, 0, keepdims=True)
    dnormed = up_now * gain_ref[...]
    dmixed = (
        dnormed
        - jnp.mean(dnormed, -1, keepdims=True)
        - normed * jnp.mean(dnormed * normed, -1, keepdims=True)
    ) * inverse
    dmixed = dmixed.astype(bf16)
    for part in range(3):
        send_ref[3072 + part * AREA : 3072 + (part + 1) * AREA, :] = dmixed[:, part * AREA : (part + 1) * AREA]
    doutt[...] = mm(out_weight_ref[...], dmixed, NT).astype(bf16)

    def backward_head(head, carry):
        at, q_unit, q_inv, q_round, k_unit, k_inv, k_round, v, factor = head_inputs(head)
        weights = exps[head]
        inverse = inv[head]
        dout = (doutt[pl.ds(at, HEAD_DIM), :].astype(f32) * inverse).astype(bf16).astype(f32)
        delta = jnp.sum(dout * hot[pl.ds(at, HEAD_DIM), :], 0, keepdims=True)
        high = delta.astype(bf16).astype(f32)
        tail = jnp.where(extra == 0, high, jnp.where(extra == 1, delta - high, 0.0))
        dout_more = jnp.concatenate([dout, tail], 0).astype(bf16)
        values = jnp.concatenate([v, jnp.where(extra < 2, -1.0, 0.0)], 0).astype(bf16)
        dscores = weights.astype(f32) * mm(values, dout_more, TN)
        dround = dscores.astype(bf16)
        dvalue = mm(weights, dout.astype(bf16), NT).T
        ones = jnp.where(extra == 0, 1.0, 0.0).astype(bf16)
        dquery = mm(jnp.concatenate([k_round, ones], 0), dround)
        excess = dquery[HEAD_DIM : HEAD_DIM + 1, :]
        dquery = dquery[:HEAD_DIM, :]
        dkey = mm(dround, q_round, NT).T
        scale_out[pl.ds(head, 1), :] = (
            jnp.sum(q_round.astype(f32) * dquery, 0, keepdims=True) - means[head] * excess
        )
        dquery = dquery * factor
        dquery = (dquery - q_unit * jnp.sum(q_unit * dquery, 0, keepdims=True)) * q_inv
        dkey = (dkey - k_unit * jnp.sum(k_unit * dkey, 0, keepdims=True)) * k_inv
        send_ref[pl.ds(768 + at, HEAD_DIM), :] = dquery.astype(bf16)
        send_ref[pl.ds(768 + D + at, HEAD_DIM), :] = dkey.astype(bf16)
        send_ref[pl.ds(768 + 2 * D + at, HEAD_DIM), :] = dvalue.astype(bf16)
        total = None
        for b in range(8):
            near = dscores[(15 - b) * 16 : (15 - b) * 16 + 16, :]
            far = dscores[(7 - b) * 16 : (7 - b) * 16 + 16, :]
            wide = jnp.concatenate(
                [near[:, :128], near[:, 128:] + far[:, :128], far[:, 128:], jnp.zeros((16, 128), f32)], 1
            )
            if b:
                wide = pltpu.roll(wide, 16 * b, 1)
            total = wide if total is None else total + wide
        table_out[head] = total
        return carry

    lax.fori_loop(0, HEADS, backward_head, 0, unroll=24)

    dtokens = up[...] + mm(weight_ref[...], send_ref[768:3072, :]).T
    grid3[...] = dtokens.reshape(WIN, WIN, D)
    pieces = [grid3[r : r + 8, c : c + 8, :].reshape(QUAD, D).astype(bf16) for r, c in places]
    d00[...] = pieces[0]
    d10[...] = pieces[2]
    dlon[0:QUAD, :] = pieces[1]
    dlon[QUAD:, :] = pieces[3]


def table_kernel(
    outer_ref, high_ref, low_ref, slope_ref, table_ref, gain_ref, scale_ref, pack_ref, rows_ref, work_ref
):
    first_coord, second_coord = slot_coords()
    lane = lax.broadcasted_iota(jnp.int32, (HEADS, 512), 1)
    first = (lane % 32) < 16
    for head in range(HEADS):
        rows_ref[:, head : head + 1, :] = table_ref[head].reshape(WIN, 1, 512)
    even = jnp.zeros((HEADS, 512), f32)
    odd = jnp.zeros((HEADS, 512), f32)
    for cj in range(WIN):
        row = rows_ref[cj]
        even = even + pltpu.roll(jnp.where(first, row, 0.0), 15 - cj, 1)
        odd = odd + pltpu.roll(jnp.where(first, 0.0, row), (512 - 1 - cj) % 512, 1)
    dgrid = jnp.concatenate([even, odd], 1)
    dlogits = dgrid * slope_ref[...]
    top = dlogits.astype(bf16).astype(f32)
    rest = dlogits - top
    pair = jnp.concatenate([top, rest], 0).astype(bf16)
    high = high_ref[...]
    outer = mm(pair, high)
    outer = outer[:HEADS] + outer[HEADS:] + mm(pair, low_ref[...])[:HEADS]
    weight = outer_ref[...]
    weight_top = weight.astype(bf16).astype(f32)
    zeros = jnp.zeros((8, SLOTS), f32)
    left = jnp.concatenate([top, rest, top, zeros], 0).astype(bf16)
    right = jnp.concatenate([weight_top, weight_top, weight - weight_top, zeros[:, :HIDDEN]], 0).astype(bf16)
    dhidden = jnp.where(high.astype(f32) > 0.0, mm(left, right, TN), 0.0)
    scale = jnp.sum(scale_ref[...], -1, keepdims=True)
    where_row = lax.broadcasted_iota(jnp.int32, (HEADS, PART), 0)
    where_lane = lax.broadcasted_iota(jnp.int32, (HEADS, PART), 1)
    first_inner = jnp.sum(first_coord * dhidden, 0, keepdims=True)
    second_inner = jnp.sum(second_coord * dhidden, 0, keepdims=True)
    offset = jnp.sum(dhidden, 0, keepdims=True)
    work_ref[0:HEADS, :] = outer[:, :PART]
    for head in range(HEADS):
        place = (head % 3) * 128
        work_ref[24 + head // 3 : 25 + head // 3, place : place + 128] = outer[head : head + 1, PART:]
    work_ref[32:33, :] = first_inner[:, :PART]
    work_ref[33:34, :] = second_inner[:, :PART]
    work_ref[34:35, :] = jnp.concatenate([first_inner[:, PART:], second_inner[:, PART:], offset[:, PART:]], 1)
    work_ref[35:36, :] = offset[:, :PART]
    work_ref[36:37, :] = gain_ref[:, :PART]
    work_ref[37:38, :] = gain_ref[:, PART:]
    work_ref[38:39, :] = jnp.sum(jnp.where(where_row == where_lane, scale, 0.0), 0, keepdims=True)
    work_ref[39:64, :] = jnp.zeros((25, PART), f32)
    pack_ref[...] = work_ref[...].astype(bf16)


def grads_kernel(keep_ref, send_ref, got_ref, pack_ref, got_pack_ref, out_ref):
    pack = pack_ref[...].astype(f32) + got_pack_ref[...].astype(f32)
    for part in range(8):
        for hi in range(2):
            total = None
            for own, source in ((keep_ref, send_ref), (got_ref, got_ref)):
                base = hi * 192 + (384 if part >= 6 else 0)
                rows = own[base : base + 192, :]
                if part < 6:
                    piece = mm(rows, source[768 + part * PART : 768 + (part + 1) * PART, :], NT)
                else:
                    first = 3072 if part == 6 else 3072 + AREA
                    halves = [
                        mm(rows, source[first + n * AREA : first + (n + 1) * AREA, :]) for n in range(2)
                    ]
                    if part == 6:
                        piece = jnp.concatenate([halves[0], halves[1][:, :128]], 1)
                    else:
                        piece = jnp.concatenate([halves[0][:, 128:], halves[1]], 1)
                total = piece if total is None else total + piece
            out_ref[hi * 8 + part] = jnp.concatenate([total, pack[part * 8 : part * 8 + 8]], 0).astype(bf16)


def plane_kernel(in_ref, out_ref):
    total = in_ref[0].astype(f32)
    for n in range(1, 16):
        total = total + in_ref[n].astype(f32)
    for z in range(8):
        out_ref[z] = jnp.concatenate([total[z * BLOCK : (z + 1) * BLOCK], total[192:200]], 0).astype(bf16)


def column_kernel(in_ref, out_ref):
    total = in_ref[0].astype(f32)
    for n in range(1, 8):
        total = total + in_ref[n].astype(f32)
    both = total.astype(bf16)
    for n in range(8):
        out_ref[n] = both


def finish_kernel(in_ref, attend_ref, output_ref, gain_ref, scale_ref, inner_ref, offset_ref, outer_ref, work_ref):
    for part in range(8):
        piece = in_ref[part].astype(f32)
        if part < 6:
            attend_ref[:, part * PART : (part + 1) * PART] = piece[:BLOCK]
        else:
            output_ref[:, (part - 6) * PART : (part - 5) * PART] = piece[:BLOCK]
        work_ref[part * 8 : part * 8 + 8, :] = piece[24:32]
    tails = [
        work_ref[24 + head // 3 : 25 + head // 3, (head % 3) * 128 : (head % 3) * 128 + 128] for head in range(HEADS)
    ]
    outer = jnp.concatenate([work_ref[0:HEADS, :], jnp.concatenate(tails, 0)], 1)
    outer_ref[...] = outer
    inner_ref[0:1, :PART] = work_ref[32:33, :]
    inner_ref[1:2, :PART] = work_ref[33:34, :]
    inner_ref[0:1, PART:] = work_ref[34:35, 0:128]
    inner_ref[1:2, PART:] = work_ref[34:35, 128:256]
    offset_ref[...] = jnp.concatenate([work_ref[35:36, :], work_ref[34:35, 256:]], 1).reshape(HIDDEN)
    gain_ref[...] = jnp.concatenate([work_ref[36:37, :], work_ref[37:38, :]], 1).reshape(D)
    scale_ref[...] = work_ref[38:39, :].reshape(PART)[:HEADS]


def vmem(count):
    return [pl.BlockSpec(memory_space=pltpu.VMEM)] * count


HBM = pl.BlockSpec(memory_space=pltpu.MemorySpace.HBM)
SMEM = pl.BlockSpec(memory_space=pltpu.SMEM)


def params(mib):
    return pltpu.CompilerParams(vmem_limit_bytes=mib * 1024 * 1024)


def cost(micros):
    return pl.CostEstimate(flops=int(micros * 1.15e9), bytes_accessed=0, transcendentals=0)


def place_of(lat, hi, z, core):
    return lat * 32 + hi * 16 + z * 2 + core


def shift_pairs(lat_step, lon_step):
    return [
        (lat * 32 + lon, ((lat + lat_step) % 8) * 32 + (lon + lon_step) % 32)
        for lat in range(8)
        for lon in range(32)
    ]


PLANE = [[place_of(lat, hi, z, core) for hi in range(2) for lat in range(8)] for z in range(8) for core in range(2)]
COLUMN = [[place_of(lat, hi, z, core) for z in range(8)] for lat in range(8) for hi in range(2) for core in range(2)]
LATS = [[place_of(lat, hi, z, core) for lat in range(8)] for hi in range(2) for z in range(8) for core in range(2)]
CORES = [
    (place_of(lat, hi, z, core), place_of(lat, hi, z, 1 - core))
    for lat in range(8)
    for hi in range(2)
    for z in range(8)
    for core in range(2)
]


def exchange(value, groups):
    return lax.all_to_all(value, BOTH, 0, 0, axis_index_groups=groups, tiled=True)


def per_device(
    features, upstream, attend_weight, output_weight, norm_gain, logit_scale,
    table_inner, table_offset, table_outer, validity,
):
    steps = ((0, 0), (0, 1), (1, 0), (1, 1))
    both = pl.pallas_call(
        cut_kernel,
        out_shape=(jax.ShapeDtypeStruct((2 * QUAD, D), bf16),) * 4,
        in_specs=[HBM] * 2,
        out_specs=tuple(vmem(4)),
        scratch_shapes=[pltpu.VMEM((WIN, WIN, D), bf16)] * 2 + [pltpu.SemaphoreType.DMA((2,))],
        compiler_params=params(60),
        cost_estimate=cost(2),
        name="cut",
    )(features, upstream)
    moved = [both[0], None, None, None]
    for n in (3, 2, 1):
        moved[n] = lax.ppermute(both[n], BOTH, shift_pairs(-steps[n][0], -steps[n][1]))

    outer_t = table_outer.T
    offset_row = table_offset.reshape(1, HIDDEN)
    last = (lax.axis_index("lat") == lax.axis_size("lat") - 1).astype(jnp.int32).reshape(1)
    core = (lax.axis_index("lon") % 2).astype(jnp.int32).reshape(1)
    bias, mask, factor, hidden_high, hidden_low, slope, gain_row = pl.pallas_call(
        bias_kernel,
        out_shape=(
            jax.ShapeDtypeStruct((HEADS, WIN, 512), f32),
            jax.ShapeDtypeStruct((AREA, AREA), f32),
            jax.ShapeDtypeStruct((HEADS, 1, AREA), f32),
            jax.ShapeDtypeStruct((SLOTS, HIDDEN), bf16),
            jax.ShapeDtypeStruct((SLOTS, HIDDEN), bf16),
            jax.ShapeDtypeStruct((HEADS, SLOTS), f32),
            jax.ShapeDtypeStruct((1, D), f32),
        ),
        in_specs=[SMEM] * 2 + vmem(5),
        out_specs=tuple(vmem(7)),
        scratch_shapes=[pltpu.VMEM((WIN, HEADS, 512), f32)],
        compiler_params=params(16),
        cost_estimate=cost(2),
        name="bias",
    )(last, logit_scale, table_inner, offset_row, outer_t, validity, norm_gain)

    quad_shape = jax.ShapeDtypeStruct((QUAD, D), bf16)
    send, keep, d00, d10, dlon, gain_part, scale_part, table_part = pl.pallas_call(
        window_kernel,
        out_shape=(
            jax.ShapeDtypeStruct((3840, AREA), bf16),
            jax.ShapeDtypeStruct((768, AREA), bf16),
            quad_shape,
            quad_shape,
            jax.ShapeDtypeStruct((2 * QUAD, D), bf16),
            jax.ShapeDtypeStruct((1, D), f32),
            jax.ShapeDtypeStruct((HEADS, AREA), f32),
            jax.ShapeDtypeStruct((HEADS, WIN, 512), f32),
        ),
        in_specs=[SMEM] + vmem(10),
        out_specs=tuple(vmem(8)),
        scratch_shapes=[
            pltpu.VMEM((WIN, WIN, D), f32),
            pltpu.VMEM((AREA, D), f32),
            pltpu.VMEM((D, AREA), f32),
            pltpu.VMEM((3 * D, AREA), f32),
            pltpu.VMEM((HEADS, AREA, AREA), bf16),
            pltpu.VMEM((HEADS, 1, AREA), f32),
            pltpu.VMEM((D, AREA), f32),
            pltpu.VMEM((D, AREA), bf16),
            pltpu.VMEM((HEADS, 1, AREA), f32),
        ],
        compiler_params=params(36),
        cost_estimate=cost(17),
        name="window",
    )(core, factor, bias, mask, *moved, gain_row, attend_weight, output_weight)

    got = lax.ppermute(send, BOTH, CORES)
    pack = pl.pallas_call(
        table_kernel,
        out_shape=jax.ShapeDtypeStruct((64, PART), bf16),
        in_specs=vmem(7),
        out_specs=vmem(1)[0],
        scratch_shapes=[pltpu.VMEM((WIN, HEADS, 512), f32), pltpu.VMEM((64, PART), f32)],
        compiler_params=params(16),
        cost_estimate=cost(5),
        name="table",
    )(outer_t, hidden_high, hidden_low, slope, table_part, gain_part, scale_part)
    got_pack = lax.ppermute(pack, BOTH, CORES)
    from_lon = lax.ppermute(dlon, BOTH, shift_pairs(0, 1))
    got_pack, from_lon = lax.optimization_barrier((got_pack, from_lon))
    grads = pl.pallas_call(
        grads_kernel,
        out_shape=jax.ShapeDtypeStruct((16, 200, PART), bf16),
        in_specs=vmem(5),
        out_specs=vmem(1)[0],
        compiler_params=params(24),
        cost_estimate=cost(2),
        name="grads",
    )(keep, send, got, pack, got_pack)
    plane = pl.pallas_call(
        plane_kernel,
        out_shape=jax.ShapeDtypeStruct((8, 32, PART), bf16),
        in_specs=vmem(1),
        out_specs=vmem(1)[0],
        compiler_params=params(16),
        cost_estimate=cost(1),
        name="plane",
    )(exchange(grads, PLANE))
    plane, d10, from_lon = lax.optimization_barrier((plane, d10, from_lon))
    from_lat = lax.ppermute(jnp.concatenate([d10, from_lon[QUAD:]], 0), BOTH, shift_pairs(1, 0))
    column, from_lat = lax.optimization_barrier((exchange(plane, COLUMN), from_lat))
    column = pl.pallas_call(
        column_kernel,
        out_shape=jax.ShapeDtypeStruct((8, 32, PART), bf16),
        in_specs=vmem(1),
        out_specs=vmem(1)[0],
        compiler_params=params(16),
        cost_estimate=cost(1),
        name="column",
    )(column)

    back = [value.reshape(SHIFT, SHIFT, D) for value in (d00, from_lon[:QUAD], from_lat[:QUAD], from_lat[QUAD:])]
    input_delta = jnp.concatenate(
        [jnp.concatenate([back[3], back[2]], 1), jnp.concatenate([back[1], back[0]], 1)], 0
    )
    column, input_delta = lax.optimization_barrier((column, input_delta))

    attend_delta, output_delta, gain, scale, inner, offset, outer = pl.pallas_call(
        finish_kernel,
        out_shape=(
            jax.ShapeDtypeStruct((BLOCK, 3 * D), f32),
            jax.ShapeDtypeStruct((BLOCK, D), f32),
            jax.ShapeDtypeStruct((D,), f32),
            jax.ShapeDtypeStruct((HEADS,), f32),
            jax.ShapeDtypeStruct((2, HIDDEN), f32),
            jax.ShapeDtypeStruct((HIDDEN,), f32),
            jax.ShapeDtypeStruct((HEADS, HIDDEN), f32),
        ),
        in_specs=vmem(1),
        out_specs=tuple(vmem(7)),
        scratch_shapes=[pltpu.VMEM((64, PART), f32)],
        compiler_params=params(16),
        cost_estimate=cost(1),
        name="finish",
    )(exchange(column, LATS))
    return (
        input_delta,
        attend_delta,
        output_delta,
        gain,
        scale,
        inner,
        offset,
        outer.T,
    )


def solution(mesh):
    in_specs = (
        P("lat", "lon", None),
        P("lat", "lon", None),
        P(),
        P(),
        P(),
        P(),
        P(),
        P(),
        P(),
        P("lat", "lon"),
    )
    out_specs = (P("lat", "lon", None), P("lon", None), P("lon", None), P(), P(), P(), P(), P())
    return jax.shard_map(
        per_device, mesh=mesh, in_specs=in_specs, out_specs=out_specs, check_vma=False
    )
```
